256 devices in a mesh: rows: 16 (over x, y), cols: 16 (over z, core).
Axes of the slice: x: 4, y: 4, z: 8, core: 2. Of those that a mesh axis runs over, the one named last changes fastest.
Arguments:
- jacobian: float32 [32768, 192], P('rows'), may hold values from -6 to 6
- factor_cols: float32 [5, 1024, 32768], P(None, 'cols', 'rows'), may hold values from -0.13125 to 0.13125
- diag_inverse: float32 [5, 1024, 1024], P(None, 'cols'), as said below
Outputs:
- whitened: float32 [32768, 192], P('rows')
The draws below stay inside these ranges and needn't reach their ends.
Inputs may be any that keep to these rules, and one draw needn't show every extreme that they name: Each diag_inverse[j] is lower triangular with a positive diagonal.
All inputs are finite; a program needn't handle non-finite values.
Results may differ from the reference program's by a relative error of at most 0.00011.
Values sent between devices are 32-bit elements; how exact they have to be, the bound alone decides.
A program may use at most 64 MiB of HBM per device.

```python
import math
import jax
import jax.numpy as jnp
from jax import lax

BS = 1024
K = 192
NC = 5
BLOCKS = 32
NTOT = 32768


def draw_diag_inverse(key, part):
    key = jax.random.fold_in(key, 7)
    first, second = jax.random.split(key)
    diagonal = jnp.exp(jax.random.uniform(first, (NC, BS), jnp.float32, math.log(0.5), math.log(2.0)))
    lower = jax.random.normal(second, (NC, BS, BS), jnp.float32) * (0.7 / BS ** 0.5)
    row_ids = jnp.arange(BS)[:, None]
    col_ids = jnp.arange(BS)[None, :]
    strict = (row_ids > col_ids).astype(jnp.float32)
    unit = (row_ids == col_ids).astype(jnp.float32)
    return lower * strict + diagonal[:, :, None] * unit


def shard_levels(key, shape, cuts, smallest, top_value):
    gain = 1.0
    for axis_at, shards_of in cuts:
        heights = jax.random.uniform(jax.random.fold_in(jax.random.fold_in(key, 6), axis_at), (shards_of,), jnp.float32, smallest / len(cuts), top_value / len(cuts))
        gain = gain * jnp.repeat(jnp.exp(heights), shape[axis_at] // shards_of).reshape((-1,) + (1,) * (len(shape) - 1 - axis_at))
    return gain


def noise(stream_key, shape, deviation, limit, shards=(), held_as=jnp.bfloat16):
    drawn = jax.random.normal(stream_key, shape, jnp.float32) * deviation
    if len(shards) > 0:
        drawn = shard_levels(stream_key, shape, shards, -0.22, 0.18) * drawn
    return jnp.clip(drawn, min=-limit, max=limit).astype(held_as)


def setup_inputs(seed: int = 0) -> dict:
    seeds = jax.random.split(jax.random.key(seed), 4)
    jacobian = noise(seeds[0], (NTOT, K), 1.0, 6.0, ((0, 16),), jnp.float32)
    factor_cols = noise(seeds[1], (NC, BS, NTOT), (0.7 / BS ** 0.5), 0.13125, ((1, 16), (2, 16)), jnp.float32)
    diag_inverse = draw_diag_inverse(jax.random.fold_in(seeds[3], 71), 0)
    return dict(jacobian=jacobian, factor_cols=factor_cols, diag_inverse=diag_inverse)


def reference(jacobian, factor_cols, diag_inverse):
    resid = jacobian.reshape(BLOCKS, BS, K)
    block_ids = jnp.arange(BLOCKS)
    for j in range(NC):
        solved = jnp.dot(diag_inverse[j], resid[j], precision=lax.Precision.HIGHEST, preferred_element_type=jnp.float32)
        update = lax.dot_general(factor_cols[j], solved, (((0,), (0,)), ((), ())), precision=lax.Precision.HIGHEST, preferred_element_type=jnp.float32)
        update = update.reshape(BLOCKS, BS, K)
        resid = resid - jnp.where((block_ids > j)[:, None, None], update, jnp.float32(0.0))
        resid = resid.at[j].set(solved)
    return resid.reshape(NTOT, K)
```

```python
import jax
import jax.numpy as jnp
from jax import lax
from jax.experimental import pallas as pl
from jax.experimental.pallas import tpu as pltpu
from jax.sharding import PartitionSpec as P

MESH = pl.DeviceIdType.MESH
NT = (((1,), (1,)), ((), ()))
NN = (((1,), (0,)), ((), ()))


def halves(a):
    hi = a.astype(jnp.bfloat16)
    lo = (a - hi.astype(jnp.float32)).astype(jnp.bfloat16)
    return hi, lo


def dot3(a, b, dims):
    ah, al = halves(a)
    bh, bl = halves(b)

    def one(p, q):
        return lax.dot_general(p, q, dims, preferred_element_type=jnp.float32)

    return one(ah, bh) + (one(ah, bl) + one(al, bh))


def lanes(i, n=128):
    return pl.ds(pl.multiple_of(i * n, n), n)


def subl(i, n):
    return pl.ds(pl.multiple_of(i * n, n), n)


def kernel(
    jac, fac, dinv, out,
    dv, fv, jv, jt, jsv, js, x0, t1, ts, tp, xf, lt2, lt3, lt4, jtile,
    pa, ss, sb, u, rsend, rbuf,
    load_sem, pair_send, pair_recv, own_send, own_recv, fwd_send, fwd_recv,
    a_send, a_recv, b_send, b_recv, h_send, h_recv, r_send, r_recv, g_send, g_recv, o_send, o_recv,
):
    r = lax.axis_index("rows")
    c = lax.axis_index("cols")
    x = r // 4
    y = r % 4
    z = c // 2
    core = c % 2
    h = y // 2
    g = x * 2 + y % 2

    def zdev(d):
        return {"cols": ((z + d + 8) % 8) * 2 + core}

    def rdev(d):
        return {"rows": (r + d) % 16}

    partner = {"cols": c + 1 - 2 * core}
    hdev = {"rows": x * 4 + 3 - y}

    def remote(src, dst, ssem, rsem, dev):
        return pltpu.make_async_remote_copy(
            src_ref=src, dst_ref=dst, send_sem=ssem, recv_sem=rsem, device_id=dev, device_id_type=MESH
        )

    sent = []

    mine = subl(core, 64)
    load_d = pltpu.make_async_copy(dinv, dv.at[:, mine, :], load_sem.at[0])
    load_d.start()
    load_f = pltpu.make_async_copy(fac, fv.at[:, mine, :], load_sem.at[1])
    load_f.start()
    load_j = [
        pltpu.make_async_copy(jac.at[pl.ds(b * 1024 + pl.multiple_of(z * 128, 128), 128), :], jsv.at[b], load_sem.at[2 + b])
        for b in range(2)
    ]
    for cp in load_j:
        cp.start()

    @pl.when(r <= 2)
    def _():
        pltpu.make_async_copy(jac, jv, load_sem.at[4]).start()

    bar = pltpu.get_barrier_semaphore()
    for d in range(1, 16):
        pl.semaphore_signal(bar, inc=1, device_id=rdev(d), device_id_type=MESH)
    for d in range(1, 8):
        pl.semaphore_signal(bar, inc=1, device_id=zdev(d), device_id_type=MESH)
    pl.semaphore_signal(bar, inc=1, device_id=partner, device_id_type=MESH)
    pl.semaphore_wait(bar, 23)

    pair = []
    for i, (src, dst) in enumerate(
        (
            (dinv.at[0], dv.at[0, mine, :]),
            (fac.at[0], fv.at[0, mine, :]),
            (dinv.at[pl.ds(1, 4)], dv.at[pl.ds(1, 4), mine, :]),
            (fac.at[pl.ds(1, 4)], fv.at[pl.ds(1, 4), mine, :]),
        )
    ):
        cp = remote(src, dst, pair_send.at[i], pair_recv.at[i], partner)
        cp.start()
        pair.append(cp)
        sent.append(cp)

    lts = {2: lt2, 3: lt3, 4: lt4}

    def tile_copies(j, d):
        to = (r + d) % 16
        tx = to // 4
        ty = to % 4
        tg = tx * 2 + ty % 2
        th = ty // 2
        rows = pl.ds(pl.multiple_of((j % 2) * 1024 + tg * 128, 128), 128)
        a_src, a_dst = fac.at[pl.ds(0, j), :, rows], lts[j].at[:, mine, :]
        j_src = jt.at[j % 2, pl.ds(pl.multiple_of(core * 96 + th * 48, 48), 48), lanes(tg)]
        j_dst = jtile.at[j]
        return (a_src, a_dst), (j_src, j_dst)

    def send_fac(j):
        for d in range(1, 16):
            (s, t), _ = tile_copies(j, d)
            remote(s, t, own_send.at[j, 0, d], own_recv.at[j, 0], rdev(d)).start()
        (s, t), _ = tile_copies(j, 0)
        pltpu.make_async_copy(s, t, own_recv.at[j, 0]).start()

    def send_jac(j):
        for d in range(1, 16):
            _, (s, t) = tile_copies(j, d)
            remote(s, t, own_send.at[j, 1, d], own_recv.at[j, 1], rdev(d)).start()
        _, (s, t) = tile_copies(j, 0)
        pltpu.make_async_copy(s, t, own_recv.at[j, 1]).start()

    def wait_fac(j):
        pltpu.make_async_copy(lts[j].at[:, mine, :], lts[j].at[:, mine, :], own_recv.at[j, 0]).wait()

    def wait_jac(j):
        pltpu.make_async_copy(jtile.at[j], jtile.at[j], own_recv.at[j, 1]).wait()

    def wait_owner_sends(j):
        for d in range(1, 16):
            (s, t), (s2, t2) = tile_copies(j, d)
            remote(s, t, own_send.at[j, 0, d], own_recv.at[j, 0], rdev(d)).wait_send()
            remote(s2, t2, own_send.at[j, 1, d], own_recv.at[j, 1], rdev(d)).wait_send()

    @pl.when(r == 1)
    def _():
        send_fac(2)
        send_fac(3)

    @pl.when(r == 2)
    def _():
        send_fac(4)

    @pl.when(r <= 2)
    def _():
        pltpu.make_async_copy(jac, jv, load_sem.at[4]).wait()
        jt[0] = jv[0:1024, :].T

    @pl.when(r == 2)
    def _():
        send_jac(4)

    load_d.wait()
    load_f.wait()
    pair[0].wait_recv()
    pair[1].wait_recv()

    half = subl(core, 96)
    quarter = subl(h, 48)

    def t1_copy(d):
        to = (r + d) % 16
        tx = to // 4
        ty = to % 4
        tg = tx * 2 + ty % 2
        th = ty // 2
        return remote(
            t1.at[pl.ds(pl.multiple_of(th * 48, 48), 48), lanes(tg)], ts.at[1], own_send.at[0, 0, d], own_recv.at[0, 0], rdev(d)
        )

    def x0_copy(d):
        return remote(x0, xf.at[0], own_send.at[0, 1, d], own_recv.at[0, 1], rdev(d))

    @pl.when(r == 0)
    def _():
        first = dot3(jt[0, half, :], dv[0], NT)
        x0[...] = first
        t1[...] = dot3(first, fv[0, :, 1024:2048], NN)
        jt[1] = jv[1024:2048, :].T

        @pl.when(z == 0)
        def _():
            t1[...] = t1[...] - jt[1, half, :]

        for d in range(1, 16):
            t1_copy(d).start()
        for d in range(1, 16):
            x0_copy(d).start()
        ts[1] = t1[0:48, 0:128]
        xf[0] = x0[...]

    @pl.when(r == 1)
    def _():
        send_jac(2)
        jt[1] = jv[1024:2048, :].T
        send_jac(3)

    for b in range(2):
        load_j[b].wait()
        js[b] = jsv[b].T

    @pl.when(r != 0)
    def _():
        pltpu.make_async_copy(ts.at[1], ts.at[1], own_recv.at[0, 0]).wait()

    def forward(j):
        wait_fac(j)
        cp = remote(lts[j].at[:, mine, :], lts[j].at[:, mine, :], fwd_send.at[j], fwd_recv.at[j], partner)
        cp.start()
        sent.append(cp)
        return cp

    fwd = {}
    swap = {}

    def update(j):
        if j == 0:
            @pl.when(r != 0)
            def _():
                pltpu.make_async_copy(xf.at[0], xf.at[0], own_recv.at[0, 1]).wait()
        else:
            swap[j].wait_recv()
        if j == 1:
            pair[3].wait_recv()
        for b in range(2):
            part = dot3(xf[j], fv[j, :, b * 1024:(b + 1) * 1024], NN)
            if j == 0:
                u[b] = part
            else:
                u[b] = u[b] + part

    for j in range(1, 5):
        stage = []
        for d in (4, 3, 5, 2, 6, 1, 7):
            cp = remote(ts.at[j], pa.at[j - 1, d - 1], a_send.at[j - 1, d], a_recv.at[j - 1, d], zdev(d))
            cp.start()
            stage.append(cp)
        sent.extend(stage)
        if j == 1:
            fwd[2] = forward(2)
        if j == 2:
            fwd[4] = forward(4)
        update(j - 1)
        for cp in stage:
            cp.wait_recv()
        total = ts[j]
        for d in range(7):
            total = total + pa[j - 1, d]
        if j == 1:
            rest = -total
        else:
            wait_jac(j)
            rest = jtile[j] - total
        ss[j - 1] = rest
        sb[j - 1, :, lanes(g)] = rest
        stage = []
        for dx in (2, 1, 3, 0):
            for dy in (1, 0):
                if dx == 0 and dy == 0:
                    continue
                ny = h * 2 + (y % 2 + dy) % 2
                to = {"rows": ((x + dx) % 4) * 4 + ny}
                k = dx * 2 + dy
                cp = remote(ss.at[j - 1], sb.at[j - 1, :, lanes(g)], b_send.at[j - 1, k], b_recv.at[j - 1, k], to)
                cp.start()
                stage.append(cp)
        sent.extend(stage)
        if j == 1:
            fwd[3] = forward(3)
        if j < 4:
            fwd[j + 1].wait_recv()
            part = dot3(xf[0, quarter, :], lts[j + 1][0], NN)
            for m in range(1, j):
                part = part + dot3(xf[m, quarter, :], lts[j + 1][m], NN)
            tp[...] = part
        if j == 1:
            pair[2].wait_recv()
        for cp in stage:
            cp.wait_recv()
        new = dot3(sb[j - 1], dv[j], NT)
        xf[j, quarter, :] = new
        if j < 4:
            ts[j + 1] = tp[...] + dot3(new, lts[j + 1][j], NN)
        cp = remote(xf.at[j, quarter, :], xf.at[j, quarter, :], h_send.at[j], h_recv.at[j], hdev)
        cp.start()
        sent.append(cp)
        swap[j] = cp

    update(4)

    paths = ((0, -1, 4), (1, 1, 4), (0, 1, 3), (1, -1, 3))
    got = [None] * 4
    for s in range(4):
        for i, (b, way, hops) in enumerate(paths):
            if s >= hops:
                continue
            target = (z + way * (hops - s) + 8) % 8
            value = u[b, :, lanes(target)]
            if s > 0:
                got[i].wait_recv()
                value = value + rbuf[i, s - 1]
            rsend[i, s] = value
            cp = remote(rsend.at[i, s], rbuf.at[i, s], r_send.at[i, s], r_recv.at[i, s], zdev(way))
            cp.start()
            sent.append(cp)
            got[i] = cp

    def piece(b, origin):
        return out.at[b, half, lanes(origin)]

    gather = {}
    last = []

    def share(b, origin, k):
        cp = remote(piece(b, origin), piece(b, origin), o_send.at[k], o_recv.at[k], partner)
        cp.start()
        sent.append(cp)
        last.append(cp)

    def hop(i, s):
        b, way, hops = gpaths[i]
        origin = (z - way * s + 8) % 8
        cp = remote(piece(b, origin), piece(b, origin), g_send.at[i, s], g_recv.at[i, s], zdev(way))
        cp.start()
        sent.append(cp)
        gather[i] = cp

    gpaths = ((0, 1, 4), (1, -1, 4), (0, -1, 3), (1, 1, 3))
    for b in range(2):
        for i, (pb, way, hops) in enumerate(paths):
            if pb == b:
                got[i].wait_recv()
        first, second = [i for i in range(4) if paths[i][0] == b]
        total = u[b, :, lanes(z)] + rbuf[first, paths[first][2] - 1] + rbuf[second, paths[second][2] - 1]
        block = r * 2 + b
        solved = xf[jnp.minimum(block, 4)]
        updated = js[b, half, :] - total
        out[b, half, lanes(z)] = jnp.where(block < 5, solved, updated)
        for i in range(4):
            if gpaths[i][0] == b:
                hop(i, 0)
        share(b, z, b)
    k = 2
    for s in range(1, 5):
        for i in range(4):
            b, way, hops = gpaths[i]
            if s > hops:
                continue
            gather[i].wait_recv()
            if s < hops:
                hop(i, s)
            share(b, (z - way * s + 8) % 8, k)
            k += 1
    for cp in last:
        cp.wait_recv()
    for cp in sent:
        cp.wait_send()

    @pl.when(r == 0)
    def _():
        for d in range(1, 16):
            t1_copy(d).wait_send()
            x0_copy(d).wait_send()

    @pl.when(r == 1)
    def _():
        wait_owner_sends(2)
        wait_owner_sends(3)

    @pl.when(r == 2)
    def _():
        wait_owner_sends(4)


def per_device(jacobian, factor_cols, diag_inverse):
    f32 = jnp.float32
    dma = pltpu.SemaphoreType.DMA
    out = pl.pallas_call(
        kernel,
        out_shape=jax.ShapeDtypeStruct((2, 192, 1024), f32),
        in_specs=[pl.BlockSpec(memory_space=pl.ANY)] * 3,
        out_specs=pl.BlockSpec(memory_space=pltpu.VMEM),
        scratch_shapes=[
            pltpu.VMEM((5, 128, 1024), f32),
            pltpu.VMEM((5, 128, 2048), f32),
            pltpu.VMEM((2048, 192), f32),
            pltpu.VMEM((2, 192, 1024), f32),
            pltpu.VMEM((2, 128, 192), f32),
            pltpu.VMEM((2, 192, 128), f32),
            pltpu.VMEM((96, 128), f32),
            pltpu.VMEM((96, 1024), f32),
            pltpu.VMEM((5, 48, 128), f32),
            pltpu.VMEM((48, 128), f32),
            pltpu.VMEM((5, 96, 128), f32),
            pltpu.VMEM((2, 128, 128), f32),
            pltpu.VMEM((3, 128, 128), f32),
            pltpu.VMEM((4, 128, 128), f32),
            pltpu.VMEM((5, 48, 128), f32),
            pltpu.VMEM((4, 7, 48, 128), f32),
            pltpu.VMEM((4, 48, 128), f32),
            pltpu.VMEM((4, 48, 1024), f32),
            pltpu.VMEM((2, 96, 1024), f32),
            pltpu.VMEM((4, 4, 96, 128), f32),
            pltpu.VMEM((4, 4, 96, 128), f32),
            dma((5,)),
            dma((4,)), dma((4,)),
            dma((5, 2, 16)), dma((5, 2)),
            dma((5,)), dma((5,)),
            dma((4, 8)), dma((4, 8)),
            dma((4, 8)), dma((4, 8)),
            dma((5,)), dma((5,)),
            dma((4, 4)), dma((4, 4)),
            dma((4, 4)), dma((4, 4)),
            dma((16,)), dma((16,)),
        ],
        compiler_params=pltpu.CompilerParams(
            collective_id=0, has_side_effects=True, vmem_limit_bytes=48 * 1024 * 1024
        ),
        name="whiten",
    )(jacobian, factor_cols, diag_inverse)
    return jnp.transpose(out, (0, 2, 1)).reshape(2048, 192)


def solution(mesh):
    in_specs = (P("rows", None), P(None, "cols", "rows"), P(None, "cols", None))
    return jax.shard_map(
        per_device, mesh=mesh, in_specs=in_specs, out_specs=P("rows", None), check_vma=False
    )
```

```python
import jax
import jax.numpy as jnp
from jax import lax
from jax.experimental import pallas as pl
from jax.experimental.pallas import tpu as pltpu
from jax.sharding import PartitionSpec as P

MESH = pl.DeviceIdType.MESH
FAR = (10, 8, 9, 11, 6, 5, 7, 4, 14, 13, 15, 12, 2, 1, 3)
NT = (((1,), (1,)), ((), ()))
NN = (((1,), (0,)), ((), ()))


def halves(a):
    hi = a.astype(jnp.bfloat16)
    lo = (a - hi.astype(jnp.float32)).astype(jnp.bfloat16)
    return hi, lo


def dot3(a, b, dims):
    ah, al = halves(a)
    bh, bl = halves(b)

    def one(p, q):
        return lax.dot_general(p, q, dims, preferred_element_type=jnp.float32)

    return one(ah, bh) + (one(ah, bl) + one(al, bh))


def lanes(i, n=128):
    return pl.ds(pl.multiple_of(i * n, n), n)


def subl(i, n):
    return pl.ds(pl.multiple_of(i * n, n), n)


def kernel(
    jac, fac, dinv, out,
    dv, fv, jt, js, x0, t1, ts, tp, xf, lt2, lt3, lt4, jtile,
    pa, ss, sb, u, rsend, rbuf,
    load_sem, pair_send, pair_recv, own_send, own_recv, fwd_send, fwd_recv, pass_send, pass_recv,
    a_send, a_recv, b_send, b_recv, h_send, h_recv, r_send, r_recv, g_send, g_recv, o_send, o_recv,
):
    r = lax.axis_index("rows")
    c = lax.axis_index("cols")
    x = r // 4
    y = r % 4
    z = c // 2
    core = c % 2
    h = y // 2
    g = x * 2 + (y + h) % 2

    def zdev(d):
        return {"cols": ((z + d + 8) % 8) * 2 + core}

    def rdev(d):
        return {"rows": (r + d) % 16}

    partner = {"cols": c + 1 - 2 * core}
    hdev = {"rows": x * 4 + 3 - y}

    def remote(src, dst, ssem, rsem, dev):
        return pltpu.make_async_remote_copy(
            src_ref=src, dst_ref=dst, send_sem=ssem, recv_sem=rsem, device_id=dev, device_id_type=MESH
        )

    sent = []

    mine = subl(core, 64)
    first_rows = pl.ds(1024, 1024)
    load_0 = [
        pltpu.make_async_copy(dinv.at[0], dv.at[0, mine, :], load_sem.at[0]),
        pltpu.make_async_copy(fac.at[0, :, first_rows], fv.at[0, mine, first_rows], load_sem.at[1]),
    ]
    load_d = pltpu.make_async_copy(dinv.at[pl.ds(1, 4)], dv.at[pl.ds(1, 4), mine, :], load_sem.at[5])
    load_f = pltpu.make_async_copy(fac.at[pl.ds(1, 4)], fv.at[pl.ds(1, 4), mine, :], load_sem.at[6])
    load_g = pltpu.make_async_copy(fac.at[0, :, pl.ds(0, 1024)], fv.at[0, mine, pl.ds(0, 1024)], load_sem.at[7])
    for cp in load_0:
        cp.start()
    load_j = [
        pltpu.make_async_copy(
            jac.at[subl(core, 96), pl.ds(pl.multiple_of(b * 1024 + z * 128, 128), 128)], js.at[b], load_sem.at[2 + b]
        )
        for b in range(2)
    ]
    for cp in load_j:
        cp.start()

    load_jt = pltpu.make_async_copy(jac.at[subl(core, 96), :], jt, load_sem.at[4])

    @pl.when(r == 0)
    def _():
        load_jt.start()

    bar = pltpu.get_barrier_semaphore()
    for d in range(1, 16):
        pl.semaphore_signal(bar, inc=1, device_id=rdev(d), device_id_type=MESH)
    for d in range(1, 8):
        pl.semaphore_signal(bar, inc=1, device_id=zdev(d), device_id_type=MESH)
    pl.semaphore_signal(bar, inc=1, device_id=partner, device_id_type=MESH)
    pl.semaphore_wait(bar, 23)

    pair = [
        remote(src, dst, pair_send.at[i], pair_recv.at[i], partner)
        for i, (src, dst) in enumerate(
            (
                (dinv.at[0], dv.at[0, mine, :]),
                (fac.at[0, :, first_rows], fv.at[0, mine, first_rows]),
                (dinv.at[pl.ds(1, 4)], dv.at[pl.ds(1, 4), mine, :]),
                (fac.at[pl.ds(1, 4)], fv.at[pl.ds(1, 4), mine, :]),
                (fac.at[0, :, pl.ds(0, 1024)], fv.at[0, mine, pl.ds(0, 1024)]),
            )
        )
    ]
    for cp in pair[:2]:
        cp.start()
        sent.append(cp)

    lts = {2: lt2, 3: lt3, 4: lt4}
    owner_h = {2: 0, 3: 0, 4: 1}

    def fac_copy(j, k):
        tx = (x + k // 2) % 4
        ty = h * 2 + (y % 2 + k % 2) % 2
        tg = tx * 2 + (ty + h) % 2
        rows = pl.ds(pl.multiple_of((j % 2) * 1024 + tg * 128, 128), 128)
        src, dst = fac.at[pl.ds(0, j), :, rows], lts[j].at[:, mine, :]
        if k == 0:
            return pltpu.make_async_copy(src, dst, own_recv.at[j, 0])
        return remote(src, dst, own_send.at[j, 0, k], own_recv.at[j, 0], {"rows": tx * 4 + ty})

    def jac_copy(j, d):
        to = (r + d) % 16
        tx = to // 4
        ty = to % 4
        th = ty // 2
        tg = tx * 2 + (ty + th) % 2
        rows = pl.ds(pl.multiple_of((j % 2) * 1024 + tg * 128, 128), 128)
        src = jac.at[pl.ds(pl.multiple_of(core * 96 + th * 48 + z * 8, 8), 8), rows]
        if d == 0:
            return pltpu.make_async_copy(src, jtile.at[j], own_recv.at[j, 1])
        return remote(src, jtile.at[j], own_send.at[j, 1, d], own_recv.at[j, 1], rdev(d))

    def send_fac(j):
        for k in (4, 5, 2, 3, 6, 7, 1, 0):
            fac_copy(j, k).start()

    def send_jac(j):
        @pl.when(z < 6)
        def _():
            for d in range(16):
                jac_copy(j, d).start()

    def wait_fac(j):
        @pl.when(h == owner_h[j])
        def _():
            pltpu.make_async_copy(lts[j].at[:, mine, :], lts[j].at[:, mine, :], own_recv.at[j, 0]).wait()
            fac_pass(j).start()

        @pl.when(h != owner_h[j])
        def _():
            fac_pass(j).wait_recv()

    def fac_pass(j):
        return remote(lts[j].at[:, mine, :], lts[j].at[:, mine, :], pass_send.at[j], pass_recv.at[j], hdev)

    def wait_jac(j):
        @pl.when(z < 6)
        def _():
            pltpu.make_async_copy(jtile.at[j], jtile.at[j], own_recv.at[j, 1]).wait()

    def wait_owner_sends(j):
        for k in range(1, 8):
            fac_copy(j, k).wait_send()

        @pl.when(z < 6)
        def _():
            for d in range(1, 16):
                jac_copy(j, d).wait_send()

    @pl.when(r == 1)
    def _():
        send_fac(2)
        send_jac(2)
        send_fac(3)
        send_jac(3)

    @pl.when(r == 2)
    def _():
        send_fac(4)
        send_jac(4)

    for cp in load_0:
        cp.wait()
    for cp in pair[:2]:
        cp.wait_recv()

    half = subl(core, 96)
    quarter = subl(h, 48)

    def first_copy(d):
        to = (r + d) % 16
        tx = to // 4
        ty = to % 4
        th = ty // 2
        tg = tx * 2 + (ty + th) % 2
        rows = pl.ds(pl.multiple_of(th * 48, 48), 48)
        t1_cp = remote(t1.at[tg, rows], ts.at[1], own_send.at[0, 0, d], own_recv.at[0, 0], rdev(d))
        x0_cp = remote(x0.at[rows], xf.at[0, rows], own_send.at[0, 1, d], own_recv.at[0, 1], rdev(d))
        return t1_cp, x0_cp

    @pl.when(r == 0)
    def _():
        load_jt.wait()
        first = dot3(jt[:, 0:1024], dv[0], NT)
        x0[...] = first
        whole = dot3(first, fv[0, :, 1024:2048], NN)
        for i in range(8):
            t1[i] = whole[:, i * 128:(i + 1) * 128]

        @pl.when(z == 0)
        def _():
            for i in range(8):
                t1[i] = t1[i] - jt[:, 1024 + i * 128:1024 + (i + 1) * 128]

        for d in FAR:
            first_copy(d)[0].start()
        for d in FAR:
            first_copy(d)[1].start()
        ts[1] = t1[0, 0:48]
        xf[0, 0:48] = x0[0:48]

    for cp in pair[2:]:
        cp.start()
        sent.append(cp)
    for cp in (load_d, load_f, load_g):
        cp.start()
    for cp in load_j:
        cp.wait()

    @pl.when(r != 0)
    def _():
        pltpu.make_async_copy(ts.at[1], ts.at[1], own_recv.at[0, 0]).wait()

    def forward(j):
        wait_fac(j)
        cp = remote(lts[j].at[:, mine, :], lts[j].at[:, mine, :], fwd_send.at[j], fwd_recv.at[j], partner)
        cp.start()
        sent.append(cp)
        return cp

    fwd = {}
    swap = {}

    def exchange(j):
        cp = remote(xf.at[j, quarter, :], xf.at[j, quarter, :], h_send.at[j], h_recv.at[j], hdev)
        cp.start()
        sent.append(cp)
        swap[j] = cp

    def update(j):
        swap[j].wait_recv()
        if j == 0:
            for cp in (load_f, load_g):
                cp.wait()
            for cp in pair[3:]:
                cp.wait_recv()
        for b in range(2):
            part = dot3(xf[j], fv[j, :, b * 1024:(b + 1) * 1024], NN)
            for i in range(8):
                piece = part[:, i * 128:(i + 1) * 128]
                u[b, i] = piece if j == 0 else u[b, i] + piece

    for j in range(1, 5):
        stage = []
        for d in (4, 3, 5, 2, 6, 1, 7):
            cp = remote(ts.at[j], pa.at[j - 1, d - 1], a_send.at[j - 1, d], a_recv.at[j - 1, d], zdev(d))
            cp.start()
            stage.append(cp)
        sent.extend(stage)
        if j == 1:
            fwd[2] = forward(2)

            @pl.when(r != 0)
            def _():
                pltpu.make_async_copy(xf.at[0, quarter], xf.at[0, quarter], own_recv.at[0, 1]).wait()

            exchange(0)
        if j == 2:
            fwd[4] = forward(4)
            update(0)
        if j > 1:
            update(j - 1)
        for cp in stage:
            cp.wait_recv()
        total = ts[j]
        for d in range(7):
            total = total + pa[j - 1, d]
        rest = -total
        ss[j - 1] = rest
        sb[j - 1, g] = rest
        stage = []
        for dx in (2, 1, 3, 0):
            for dy in (1, 0):
                if dx == 0 and dy == 0:
                    continue
                ny = h * 2 + (y + dy) % 2
                to = {"rows": ((x + dx) % 4) * 4 + ny}
                k = dx * 2 + dy
                cp = remote(ss.at[j - 1], sb.at[j - 1, g], b_send.at[j - 1, k], b_recv.at[j - 1, k], to)
                cp.start()
                stage.append(cp)
        sent.extend(stage)
        if j == 1:
            fwd[3] = forward(3)
        if j < 4:
            fwd[j + 1].wait_recv()
            part = dot3(xf[0, quarter, :], lts[j + 1][0], NN)
            for m in range(1, j):
                part = part + dot3(xf[m, quarter, :], lts[j + 1][m], NN)
            tp[...] = part
        if j == 1:
            load_d.wait()
            pair[2].wait_recv()
        for cp in stage:
            cp.wait_recv()
        new = dot3(jnp.concatenate([sb[j - 1, i] for i in range(8)], axis=1), dv[j], NT)
        xf[j, quarter, :] = new
        if j < 4:
            ts[j + 1] = tp[...] + dot3(new, lts[j + 1][j], NN)
            wait_jac(j + 1)

            @pl.when(z < 6)
            def _():
                ts[j + 1, subl(z, 8)] = ts[j + 1, subl(z, 8)] - jtile[j + 1]
        exchange(j)

    update(4)

    paths = ((0, -1, 4), (1, 1, 4), (0, 1, 3), (1, -1, 3))
    got = [None] * 4
    for s in range(4):
        for i, (b, way, hops) in enumerate(paths):
            if s >= hops:
                continue
            target = (z + way * (hops - s) + 8) % 8
            value = u[b, target]
            if s > 0:
                got[i].wait_recv()
                value = value + rbuf[i, s - 1]
            rsend[i, s] = value
            cp = remote(rsend.at[i, s], rbuf.at[i, s], r_send.at[i, s], r_recv.at[i, s], zdev(way))
            cp.start()
            sent.append(cp)
            got[i] = cp

    def piece(b, origin):
        return out.at[b * 8 + origin, half]

    gather = {}
    last = []

    def share(b, origin, k):
        cp = remote(piece(b, origin), piece(b, origin), o_send.at[k], o_recv.at[k], partner)
        cp.start()
        sent.append(cp)
        last.append(cp)

    def hop(i, s):
        b, way, hops = gpaths[i]
        origin = (z - way * s + 8) % 8
        cp = remote(piece(b, origin), piece(b, origin), g_send.at[i, s], g_recv.at[i, s], zdev(way))
        cp.start()
        sent.append(cp)
        gather[i] = cp

    gpaths = ((0, 1, 4), (1, -1, 4), (0, -1, 3), (1, 1, 3))
    for b in range(2):
        for i, (pb, way, hops) in enumerate(paths):
            if pb == b:
                got[i].wait_recv()
        first, second = [i for i in range(4) if paths[i][0] == b]
        total = u[b, z] + rbuf[first, paths[first][2] - 1] + rbuf[second, paths[second][2] - 1]
        block = r * 2 + b
        solved = xf[jnp.minimum(block, 4)]
        updated = js[b] - total
        out[b * 8 + z, half] = jnp.where(block < 5, solved, updated)
        for i in range(4):
            if gpaths[i][0] == b:
                hop(i, 0)
        share(b, z, b)
    k = 2
    for s in range(1, 5):
        for i in range(4):
            b, way, hops = gpaths[i]
            if s > hops:
                continue
            gather[i].wait_recv()
            if s < hops:
                hop(i, s)
            share(b, (z - way * s + 8) % 8, k)
            k += 1
    for cp in last:
        cp.wait_recv()
    for cp in sent:
        cp.wait_send()

    @pl.when(r == 0)
    def _():
        for d in range(1, 16):
            for cp in first_copy(d):
                cp.wait_send()

    @pl.when(r == 1)
    def _():
        wait_owner_sends(2)
        wait_owner_sends(3)

    @pl.when(r == 2)
    def _():
        wait_owner_sends(4)

    for j in (2, 3, 4):
        @pl.when(h == owner_h[j])
        def _():
            fac_pass(j).wait_send()


def per_device(jacobian, factor_cols, diag_inverse):
    f32 = jnp.float32
    dma = pltpu.SemaphoreType.DMA
    out = pl.pallas_call(
        kernel,
        out_shape=jax.ShapeDtypeStruct((16, 192, 128), f32),
        in_specs=[pl.BlockSpec(memory_space=pl.ANY)] * 3,
        out_specs=pl.BlockSpec(memory_space=pltpu.VMEM),
        scratch_shapes=[
            pltpu.VMEM((5, 128, 1024), f32),
            pltpu.VMEM((5, 128, 2048), f32),
            pltpu.VMEM((96, 2048), f32),
            pltpu.VMEM((2, 96, 128), f32),
            pltpu.VMEM((96, 128), f32),
            pltpu.VMEM((8, 96, 128), f32),
            pltpu.VMEM((5, 48, 128), f32),
            pltpu.VMEM((48, 128), f32),
            pltpu.VMEM((5, 96, 128), f32),
            pltpu.VMEM((2, 128, 128), f32),
            pltpu.VMEM((3, 128, 128), f32),
            pltpu.VMEM((4, 128, 128), f32),
            pltpu.VMEM((5, 8, 128), f32),
            pltpu.VMEM((4, 7, 48, 128), f32),
            pltpu.VMEM((4, 48, 128), f32),
            pltpu.VMEM((4, 8, 48, 128), f32),
            pltpu.VMEM((2, 8, 96, 128), f32),
            pltpu.VMEM((4, 4, 96, 128), f32),
            pltpu.VMEM((4, 4, 96, 128), f32),
            dma((8,)),
            dma((5,)), dma((5,)),
            dma((5, 2, 16)), dma((5, 2)),
            dma((5,)), dma((5,)),
            dma((5,)), dma((5,)),
            dma((4, 8)), dma((4, 8)),
            dma((4, 8)), dma((4, 8)),
            dma((5,)), dma((5,)),
            dma((4, 4)), dma((4, 4)),
            dma((4, 4)), dma((4, 4)),
            dma((16,)), dma((16,)),
        ],
        compiler_params=pltpu.CompilerParams(
            collective_id=0, has_side_effects=True, vmem_limit_bytes=48 * 1024 * 1024
        ),
        name="whiten",
    )(jacobian.T, factor_cols, diag_inverse)
    return jnp.transpose(out, (0, 2, 1)).reshape(2048, 192)


def solution(mesh):
    in_specs = (P("rows", None), P(None, "cols", "rows"), P(None, "cols", None))
    return jax.shard_map(
        per_device, mesh=mesh, in_specs=in_specs, out_specs=P("rows", None), check_vma=False
    )
```

```python
import jax
import jax.numpy as jnp
from jax import lax
from jax.experimental import pallas as pl
from jax.experimental.pallas import tpu as pltpu
from jax.sharding import PartitionSpec as P

MESH = pl.DeviceIdType.MESH
FAR = (10, 8, 9, 11, 6, 5, 7, 4, 14, 13, 15, 12, 2, 1, 3)
NT = (((1,), (1,)), ((), ()))
NN = (((1,), (0,)), ((), ()))


def halves(a):
    hi = a.astype(jnp.bfloat16)
    lo = (a - hi.astype(jnp.float32)).astype(jnp.bfloat16)
    return hi, lo


def dot3(a, b, dims):
    ah, al = halves(a)
    bh, bl = halves(b)

    def one(p, q):
        return lax.dot_general(p, q, dims, preferred_element_type=jnp.float32)

    return one(ah, bh) + (one(ah, bl) + one(al, bh))


def lanes(i, n=128):
    return pl.ds(pl.multiple_of(i * n, n), n)


def subl(i, n):
    return pl.ds(pl.multiple_of(i * n, n), n)


def kernel(
    jac, fac, dinv, out,
    dv, fv, jt, js, x0, t1, tpart, tin, stage_f, ts, tp, xf, lt2, lt3, lt4, jtile,
    pa, ss, sb, u, rsend, rbuf, og,
    load_sem, pair_send, pair_recv, own_send, own_recv, fwd_send, fwd_recv, pass_send, pass_recv,
    a_send, a_recv, b_send, b_recv, h_send, h_recv, r_send, r_recv, g_send, g_recv, o_send, o_recv,
):
    r = lax.axis_index("rows")
    c = lax.axis_index("cols")
    x = r // 4
    y = r % 4
    z = c // 2
    core = c % 2
    h = y // 2
    g = x * 2 + (y + h) % 2

    def zdev(d):
        return {"cols": ((z + d + 8) % 8) * 2 + core}

    def rdev(d):
        return {"rows": (r + d) % 16}

    partner = {"cols": c + 1 - 2 * core}
    hdev = {"rows": x * 4 + 3 - y}

    def remote(src, dst, ssem, rsem, dev):
        return pltpu.make_async_remote_copy(
            src_ref=src, dst_ref=dst, send_sem=ssem, recv_sem=rsem, device_id=dev, device_id_type=MESH
        )

    sent = []

    bar = pltpu.get_barrier_semaphore()
    for d in range(1, 16):
        pl.semaphore_signal(bar, inc=1, device_id=rdev(d), device_id_type=MESH)
    for d in range(1, 8):
        pl.semaphore_signal(bar, inc=1, device_id=zdev(d), device_id_type=MESH)
    pl.semaphore_signal(bar, inc=1, device_id=partner, device_id_type=MESH)

    mine = subl(core, 64)
    first_rows = pl.ds(1024, 1024)
    load_0 = [
        pltpu.make_async_copy(dinv.at[0], dv.at[0, mine, :], load_sem.at[0]),
        pltpu.make_async_copy(fac.at[0, :, first_rows], fv.at[0, mine, first_rows], load_sem.at[1]),
    ]
    load_d = pltpu.make_async_copy(dinv.at[pl.ds(1, 4)], dv.at[pl.ds(1, 4), mine, :], load_sem.at[5])
    load_f = pltpu.make_async_copy(fac.at[pl.ds(1, 4)], fv.at[pl.ds(1, 4), mine, :], load_sem.at[6])
    load_g = pltpu.make_async_copy(fac.at[0, :, pl.ds(0, 1024)], fv.at[0, mine, pl.ds(0, 1024)], load_sem.at[7])
    for cp in load_0:
        cp.start()
    load_j = [
        pltpu.make_async_copy(
            jac.at[subl(core, 96), pl.ds(pl.multiple_of(b * 1024 + z * 128, 128), 128)], js.at[b], load_sem.at[2 + b]
        )
        for b in range(2)
    ]
    for cp in load_j:
        cp.start()

    load_jt = pltpu.make_async_copy(jac, jt, load_sem.at[4])

    @pl.when(r == 0)
    def _():
        load_jt.start()
        for cp in load_0:
            cp.wait()
        load_jt.wait()
        first = dot3(jt[:, 0:1024], dv[0, mine, :], NT)
        whole = dot3(first, fv[0, mine, 1024:2048], NN)
        for i in range(8):
            for k in range(2):
                tpart[k, i] = whole[k * 96:(k + 1) * 96, i * 128:(i + 1) * 128]

        @pl.when(c == 0)
        def _():
            for i in range(8):
                for k in range(2):
                    tpart[k, i] = tpart[k, i] - jt[k * 96:(k + 1) * 96, 1024 + i * 128:1024 + (i + 1) * 128]

    lts = {2: lt2, 3: lt3, 4: lt4}
    owner_h = {2: 0, 3: 0, 4: 1}

    def fac_copy(j, k, fetch=False):
        tx = (x + k // 2) % 4
        ty = h * 2 + (y % 2 + k % 2) % 2
        tg = tx * 2 + (ty + h) % 2
        rows = pl.ds(pl.multiple_of((j % 2) * 1024 + tg * 128, 128), 128)
        dst = lts[j].at[:, mine, :]
        part = stage_f.at[pl.ds(0 if j == 4 else 3 * (j - 2), j), k]
        if fetch:
            return pltpu.make_async_copy(fac.at[pl.ds(0, j), :, rows], dst if k == 0 else part, own_send.at[j, 0, k] if k else own_recv.at[j, 0])
        return remote(part, dst, own_send.at[j, 0, k], own_recv.at[j, 0], {"rows": tx * 4 + ty})

    def jac_copy(j, d):
        to = (r + d) % 16
        tx = to // 4
        ty = to % 4
        th = ty // 2
        tg = tx * 2 + (ty + th) % 2
        rows = pl.ds(pl.multiple_of((j % 2) * 1024 + tg * 128, 128), 128)
        src = jac.at[pl.ds(pl.multiple_of(core * 96 + th * 48 + z * 8, 8), 8), rows]
        if d == 0:
            return pltpu.make_async_copy(src, jtile.at[j], own_recv.at[j, 1])
        return remote(src, jtile.at[j], own_send.at[j, 1, d], own_recv.at[j, 1], rdev(d))

    def fetch_fac(j):
        for k in (4, 5, 2, 3, 6, 7, 1, 0):
            fac_copy(j, k, True).start()

    def send_fac(j):
        for k in (4, 5, 2, 3, 6, 7, 1):
            fac_copy(j, k, True).wait()
            fac_copy(j, k).start()

    def send_jac(j):
        @pl.when(z < 6)
        def _():
            for d in range(16):
                jac_copy(j, d).start()

    def wait_fac(j):
        @pl.when(h == owner_h[j])
        def _():
            pltpu.make_async_copy(lts[j].at[:, mine, :], lts[j].at[:, mine, :], own_recv.at[j, 0]).wait()
            fac_pass(j).start()

        @pl.when(h != owner_h[j])
        def _():
            fac_pass(j).wait_recv()

    def fac_pass(j):
        return remote(lts[j].at[:, mine, :], lts[j].at[:, mine, :], pass_send.at[j], pass_recv.at[j], hdev)

    def wait_jac(j):
        @pl.when(z < 6)
        def _():
            pltpu.make_async_copy(jtile.at[j], jtile.at[j], own_recv.at[j, 1]).wait()

    def wait_owner_sends(j):
        for k in range(1, 8):
            fac_copy(j, k).wait_send()

        @pl.when(z < 6)
        def _():
            for d in range(1, 16):
                jac_copy(j, d).wait_send()

    @pl.when(r == 1)
    def _():
        fetch_fac(2)
        fetch_fac(3)

    @pl.when(r == 2)
    def _():
        fetch_fac(4)

    pl.semaphore_wait(bar, 23)
    swap_t = remote(tpart.at[1 - core], tin, pair_send.at[5], pair_recv.at[5], partner)

    @pl.when(r == 0)
    def _():
        swap_t.start()

    pair = [
        remote(src, dst, pair_send.at[i], pair_recv.at[i], partner)
        for i, (src, dst) in enumerate(
            (
                (dinv.at[0], dv.at[0, mine, :]),
                (fac.at[0, :, first_rows], fv.at[0, mine, first_rows]),
                (dinv.at[pl.ds(1, 4)], dv.at[pl.ds(1, 4), mine, :]),
                (fac.at[pl.ds(1, 4)], fv.at[pl.ds(1, 4), mine, :]),
                (fac.at[0, :, pl.ds(0, 1024)], fv.at[0, mine, pl.ds(0, 1024)]),
            )
        )
    ]
    for cp in pair[:2]:
        cp.start()
        sent.append(cp)

    @pl.when(r == 1)
    def _():
        send_fac(2)
        send_jac(2)
        send_fac(3)
        send_jac(3)

    @pl.when(r == 2)
    def _():
        send_fac(4)
        send_jac(4)

    @pl.when(r != 0)
    def _():
        for cp in load_0:
            cp.wait()

    half = subl(core, 96)
    quarter = subl(h, 48)

    def first_copy(d):
        to = (r + d) % 16
        tx = to // 4
        ty = to % 4
        th = ty // 2
        tg = tx * 2 + (ty + th) % 2
        rows = pl.ds(pl.multiple_of(th * 48, 48), 48)
        t1_cp = remote(t1.at[tg, rows], ts.at[1], own_send.at[0, 0, d], own_recv.at[0, 0], rdev(d))
        x0_cp = remote(x0.at[rows], xf.at[0, rows], own_send.at[0, 1, d], own_recv.at[0, 1], rdev(d))
        return t1_cp, x0_cp

    @pl.when(r == 0)
    def _():
        swap_t.wait_recv()
        for i in range(8):
            t1[i] = tpart[core, i] + tin[i]
        for d in FAR:
            first_copy(d)[0].start()
        ts[1] = t1[0, 0:48]
        pair[0].wait_recv()
        x0[...] = dot3(jt[half, 0:1024], dv[0], NT)
        for d in FAR:
            first_copy(d)[1].start()
        xf[0, 0:48] = x0[0:48]

    @pl.when(r != 0)
    def _():
        pair[0].wait_recv()

    for cp in pair[2:]:
        cp.start()
        sent.append(cp)
    for cp in (load_d, load_f, load_g):
        cp.start()
    for cp in load_j:
        cp.wait()

    @pl.when(r != 0)
    def _():
        pltpu.make_async_copy(ts.at[1], ts.at[1], own_recv.at[0, 0]).wait()

    def forward(j):
        wait_fac(j)
        cp = remote(lts[j].at[:, mine, :], lts[j].at[:, mine, :], fwd_send.at[j], fwd_recv.at[j], partner)
        cp.start()
        sent.append(cp)
        return cp

    fwd = {}
    swap = {}

    def exchange(j):
        cp = remote(xf.at[j, quarter, :], xf.at[j, quarter, :], h_send.at[j], h_recv.at[j], hdev)
        cp.start()
        sent.append(cp)
        swap[j] = cp

    def update(j):
        swap[j].wait_recv()
        if j == 0:
            for cp in (load_f, load_g):
                cp.wait()
            for cp in (pair[1], pair[3], pair[4]):
                cp.wait_recv()
        for b in range(2):
            part = dot3(xf[j], fv[j, :, b * 1024:(b + 1) * 1024], NN)
            for i in range(8):
                piece = part[:, i * 128:(i + 1) * 128]
                u[b, i] = piece if j == 0 else u[b, i] + piece

    for j in range(1, 5):
        stage = []
        for d in (4, 3, 5, 2, 6, 1, 7):
            cp = remote(ts.at[j], pa.at[j - 1, d - 1], a_send.at[j - 1, d], a_recv.at[j - 1, d], zdev(d))
            cp.start()
            stage.append(cp)
        sent.extend(stage)
        if j == 1:
            fwd[2] = forward(2)

            @pl.when(r != 0)
            def _():
                pltpu.make_async_copy(xf.at[0, quarter], xf.at[0, quarter], own_recv.at[0, 1]).wait()

            exchange(0)
        if j == 2:
            fwd[4] = forward(4)
            update(0)
        if j > 1:
            update(j - 1)
        for cp in stage:
            cp.wait_recv()
        total = ts[j]
        for d in range(7):
            total = total + pa[j - 1, d]
        rest = -total
        ss[j - 1] = rest
        sb[j - 1, g] = rest
        stage = []
        for dx in (2, 1, 3, 0):
            for dy in (1, 0):
                if dx == 0 and dy == 0:
                    continue
                ny = h * 2 + (y + dy) % 2
                to = {"rows": ((x + dx) % 4) * 4 + ny}
                k = dx * 2 + dy
                cp = remote(ss.at[j - 1], sb.at[j - 1, g], b_send.at[j - 1, k], b_recv.at[j - 1, k], to)
                cp.start()
                stage.append(cp)
        sent.extend(stage)
        if j == 1:
            fwd[3] = forward(3)
        if j < 4:
            fwd[j + 1].wait_recv()
            part = dot3(xf[0, quarter, :], lts[j + 1][0], NN)
            for m in range(1, j):
                part = part + dot3(xf[m, quarter, :], lts[j + 1][m], NN)
            tp[...] = part
        if j == 1:
            load_d.wait()
            pair[2].wait_recv()
        for cp in stage:
            cp.wait_recv()
        new = dot3(jnp.concatenate([sb[j - 1, i] for i in range(8)], axis=1), dv[j], NT)
        xf[j, quarter, :] = new
        if j < 4:
            ts[j + 1] = tp[...] + dot3(new, lts[j + 1][j], NN)
            wait_jac(j + 1)

            @pl.when(z < 6)
            def _():
                ts[j + 1, subl(z, 8)] = ts[j + 1, subl(z, 8)] - jtile[j + 1]
        exchange(j)

    update(4)

    paths = ((0, -1, 4), (1, 1, 4), (0, 1, 3), (1, -1, 3))
    got = [None] * 4
    for s in range(4):
        for i, (b, way, hops) in enumerate(paths):
            if s >= hops:
                continue
            target = (z + way * (hops - s) + 8) % 8
            value = u[b, target]
            if s > 0:
                got[i].wait_recv()
                value = value + rbuf[i, s - 1]
            rsend[i, s] = value
            cp = remote(rsend.at[i, s], rbuf.at[i, s], r_send.at[i, s], r_recv.at[i, s], zdev(way))
            cp.start()
            sent.append(cp)
            got[i] = cp

    def piece(b, origin):
        return og.at[b * 8 + origin]

    gather = {}

    def hop(i, s):
        b, way, hops = gpaths[i]
        origin = (z - way * s + 8) % 8
        cp = remote(piece(b, origin), piece(b, origin), g_send.at[i, s], g_recv.at[i, s], zdev(way))
        cp.start()
        sent.append(cp)
        gather[i] = cp

    gpaths = ((0, 1, 4), (1, -1, 4), (0, -1, 3), (1, 1, 3))
    for b in range(2):
        for i, (pb, way, hops) in enumerate(paths):
            if pb == b:
                got[i].wait_recv()
        first, second = [i for i in range(4) if paths[i][0] == b]
        total = u[b, z] + rbuf[first, paths[first][2] - 1] + rbuf[second, paths[second][2] - 1]
        block = r * 2 + b
        solved = xf[jnp.minimum(block, 4)]
        updated = js[b] - total
        og[b * 8 + z] = jnp.where(block < 5, solved, updated)
        for i in range(4):
            if gpaths[i][0] == b:
                hop(i, 0)
    for s in range(1, 5):
        for i in range(4):
            b, way, hops = gpaths[i]
            if s > hops:
                continue
            gather[i].wait_recv()
            if s < hops:
                hop(i, s)
    last = remote(og, out.at[:, half], o_send, o_recv, partner)
    last.start()
    sent.append(last)
    keep = pltpu.make_async_copy(og, out.at[:, half], load_sem.at[8])
    keep.start()
    keep.wait()
    last.wait_recv()
    for cp in sent:
        cp.wait_send()

    @pl.when(r == 0)
    def _():
        swap_t.wait_send()
        for d in range(1, 16):
            for cp in first_copy(d):
                cp.wait_send()

    @pl.when(r == 1)
    def _():
        wait_owner_sends(2)
        wait_owner_sends(3)

    @pl.when(r == 2)
    def _():
        wait_owner_sends(4)

    for j in (2, 3, 4):
        @pl.when(h == owner_h[j])
        def _():
            fac_pass(j).wait_send()


def per_device(jacobian, factor_cols, diag_inverse):
    f32 = jnp.float32
    dma = pltpu.SemaphoreType.DMA
    out = pl.pallas_call(
        kernel,
        out_shape=jax.ShapeDtypeStruct((16, 192, 128), f32),
        in_specs=[pl.BlockSpec(memory_space=pltpu.HBM)] * 3,
        out_specs=pl.BlockSpec(memory_space=pltpu.HBM),
        scratch_shapes=[
            pltpu.VMEM((5, 128, 1024), f32),
            pltpu.VMEM((5, 128, 2048), f32),
            pltpu.VMEM((192, 2048), f32),
            pltpu.VMEM((2, 96, 128), f32),
            pltpu.VMEM((96, 128), f32),
            pltpu.VMEM((8, 96, 128), f32),
            pltpu.VMEM((2, 8, 96, 128), f32),
            pltpu.VMEM((8, 96, 128), f32),
            pltpu.VMEM((6, 8, 64, 128), f32),
            pltpu.VMEM((5, 48, 128), f32),
            pltpu.VMEM((48, 128), f32),
            pltpu.VMEM((5, 96, 128), f32),
            pltpu.VMEM((2, 128, 128), f32),
            pltpu.VMEM((3, 128, 128), f32),
            pltpu.VMEM((4, 128, 128), f32),
            pltpu.VMEM((5, 8, 128), f32),
            pltpu.VMEM((4, 7, 48, 128), f32),
            pltpu.VMEM((4, 48, 128), f32),
            pltpu.VMEM((4, 8, 48, 128), f32),
            pltpu.VMEM((2, 8, 96, 128), f32),
            pltpu.VMEM((4, 4, 96, 128), f32),
            pltpu.VMEM((4, 4, 96, 128), f32),
            pltpu.VMEM((16, 96, 128), f32),
            dma((9,)),
            dma((6,)), dma((6,)),
            dma((5, 2, 16)), dma((5, 2)),
            dma((5,)), dma((5,)),
            dma((5,)), dma((5,)),
            dma((4, 8)), dma((4, 8)),
            dma((4, 8)), dma((4, 8)),
            dma((5,)), dma((5,)),
            dma((4, 4)), dma((4, 4)),
            dma((4, 4)), dma((4, 4)),
            dma(()), dma(()),
        ],
        compiler_params=pltpu.CompilerParams(
            collective_id=0, has_side_effects=True, vmem_limit_bytes=57 * 1024 * 1024
        ),
        name="whiten",
    )(jacobian.T, factor_cols, diag_inverse)
    return jnp.transpose(out, (0, 2, 1)).reshape(2048, 192)


def solution(mesh):
    in_specs = (P("rows", None), P(None, "cols", "rows"), P(None, "cols", None))
    return jax.shard_map(
        per_device, mesh=mesh, in_specs=in_specs, out_specs=P("rows", None), check_vma=False
    )
```

```python
import jax
import jax.numpy as jnp
from jax import lax
from jax.experimental import pallas as pl
from jax.experimental.pallas import tpu as pltpu
from jax.sharding import PartitionSpec as P

MESH = pl.DeviceIdType.MESH
FAR = (10, 8, 9, 11, 6, 5, 7, 4, 14, 13, 15, 12, 2, 1, 3)
NT = (((1,), (1,)), ((), ()))
NN = (((1,), (0,)), ((), ()))


def halves(a):
    hi = a.astype(jnp.bfloat16)
    lo = (a - hi.astype(jnp.float32)).astype(jnp.bfloat16)
    return hi, lo


def dot3(a, b, dims):
    ah, al = halves(a)
    bh, bl = halves(b)

    def one(p, q):
        return lax.dot_general(p, q, dims, preferred_element_type=jnp.float32)

    return one(ah, bh) + (one(ah, bl) + one(al, bh))


def lanes(i, n=128):
    return pl.ds(pl.multiple_of(i * n, n), n)


def subl(i, n):
    return pl.ds(pl.multiple_of(i * n, n), n)


def kernel(
    jac, fac, dinv, out,
    dv, fv, jt, js, x0, t1, tpart, tin, stage_f, ts, tp, xf, lt2, lt3, lt4, jtile,
    pa, ss, sb, u, rsend, rbuf, og, g4, xz,
    load_sem, pair_send, pair_recv, own_send, own_recv, fwd_send, fwd_recv, pass_send, pass_recv,
    a_send, a_recv, b_send, b_recv, h_send, h_recv, r_send, r_recv, g_send, g_recv, o_send, o_recv, z_send, z_recv, x_send, x_recv,
):
    r = lax.axis_index("rows")
    c = lax.axis_index("cols")
    x = r // 4
    y = r % 4
    z = c // 2
    core = c % 2
    h = y // 2
    g = x * 2 + (y + h) % 2

    def zdev(d):
        return {"cols": ((z + d + 8) % 8) * 2 + core}

    def rdev(d):
        return {"rows": (r + d) % 16}

    partner = {"cols": c + 1 - 2 * core}
    hdev = {"rows": x * 4 + 3 - y}

    def remote(src, dst, ssem, rsem, dev):
        return pltpu.make_async_remote_copy(
            src_ref=src, dst_ref=dst, send_sem=ssem, recv_sem=rsem, device_id=dev, device_id_type=MESH
        )

    sent = []

    bar = pltpu.get_barrier_semaphore()
    for d in range(1, 16):
        pl.semaphore_signal(bar, inc=1, device_id=rdev(d), device_id_type=MESH)
    for d in range(1, 8):
        pl.semaphore_signal(bar, inc=1, device_id=zdev(d), device_id_type=MESH)
    pl.semaphore_signal(bar, inc=1, device_id=partner, device_id_type=MESH)

    mine = subl(core, 64)
    first_rows = pl.ds(1024, 1024)
    load_0 = [
        pltpu.make_async_copy(dinv.at[0], dv.at[0, mine, :], load_sem.at[0]),
        pltpu.make_async_copy(fac.at[0, :, first_rows], fv.at[0, mine, first_rows], load_sem.at[1]),
    ]
    load_d = pltpu.make_async_copy(dinv.at[pl.ds(1, 4)], dv.at[pl.ds(1, 4), mine, :], load_sem.at[5])
    load_f = pltpu.make_async_copy(fac.at[pl.ds(1, 3)], fv.at[pl.ds(1, 3), mine, :], load_sem.at[6])
    load_g = pltpu.make_async_copy(fac.at[0, :, pl.ds(0, 1024)], fv.at[0, mine, pl.ds(0, 1024)], load_sem.at[7])
    for cp in load_0:
        cp.start()
    load_j = [
        pltpu.make_async_copy(
            jac.at[subl(core, 96), pl.ds(pl.multiple_of(b * 1024 + z * 128, 128), 128)], js.at[b], load_sem.at[2 + b]
        )
        for b in range(2)
    ]
    for cp in load_j:
        cp.start()

    load_jt = pltpu.make_async_copy(jac, jt, load_sem.at[4])

    @pl.when(r == 0)
    def _():
        load_jt.start()
        for cp in load_0:
            cp.wait()
        load_jt.wait()
        first = dot3(jt[:, 0:1024], dv[0, mine, :], NT)
        whole = dot3(first, fv[0, mine, 1024:2048], NN)
        for i in range(8):
            for k in range(2):
                tpart[k, i] = whole[k * 96:(k + 1) * 96, i * 128:(i + 1) * 128]

        @pl.when(c == 0)
        def _():
            for i in range(8):
                for k in range(2):
                    tpart[k, i] = tpart[k, i] - jt[k * 96:(k + 1) * 96, 1024 + i * 128:1024 + (i + 1) * 128]

    lts = {2: lt2, 3: lt3, 4: lt4}
    owner_h = {2: 0, 3: 0, 4: 1}

    def fac_copy(j, k, fetch=False):
        tx = (x + k // 2) % 4
        ty = h * 2 + (y % 2 + k % 2) % 2
        tg = tx * 2 + (ty + h) % 2
        rows = pl.ds(pl.multiple_of((j % 2) * 1024 + tg * 128, 128), 128)
        dst = lts[j].at[:, mine, :]
        part = stage_f.at[pl.ds(0 if j == 4 else 3 * (j - 2), j), k]
        if fetch:
            return pltpu.make_async_copy(fac.at[pl.ds(0, j), :, rows], dst if k == 0 else part, own_send.at[j, 0, k] if k else own_recv.at[j, 0])
        return remote(part, dst, own_send.at[j, 0, k], own_recv.at[j, 0], {"rows": tx * 4 + ty})

    def jac_copy(j, d):
        to = (r + d) % 16
        tx = to // 4
        ty = to % 4
        th = ty // 2
        tg = tx * 2 + (ty + th) % 2
        rows = pl.ds(pl.multiple_of((j % 2) * 1024 + tg * 128, 128), 128)
        src = jac.at[pl.ds(pl.multiple_of(core * 96 + th * 48 + z * 8, 8), 8), rows]
        if d == 0:
            return pltpu.make_async_copy(src, jtile.at[j], own_recv.at[j, 1])
        return remote(src, jtile.at[j], own_send.at[j, 1, d], own_recv.at[j, 1], rdev(d))

    def fetch_fac(j):
        for k in (4, 5, 2, 3, 6, 7, 1, 0):
            fac_copy(j, k, True).start()

    def send_fac(j):
        for k in (4, 5, 2, 3, 6, 7, 1):
            fac_copy(j, k, True).wait()
            fac_copy(j, k).start()

    def send_jac(j):
        @pl.when(z < 6)
        def _():
            for d in range(16):
                jac_copy(j, d).start()

    def wait_fac(j):
        @pl.when(h == owner_h[j])
        def _():
            pltpu.make_async_copy(lts[j].at[:, mine, :], lts[j].at[:, mine, :], own_recv.at[j, 0]).wait()
            fac_pass(j).start()

        @pl.when(h != owner_h[j])
        def _():
            fac_pass(j).wait_recv()

    def fac_pass(j):
        return remote(lts[j].at[:, mine, :], lts[j].at[:, mine, :], pass_send.at[j], pass_recv.at[j], hdev)

    def wait_jac(j):
        @pl.when(z < 6)
        def _():
            pltpu.make_async_copy(jtile.at[j], jtile.at[j], own_recv.at[j, 1]).wait()

    def wait_owner_sends(j):
        for k in range(1, 8):
            fac_copy(j, k).wait_send()

        @pl.when(z < 6)
        def _():
            for d in range(1, 16):
                jac_copy(j, d).wait_send()

    @pl.when(r == 1)
    def _():
        fetch_fac(2)
        fetch_fac(3)

    @pl.when(r == 2)
    def _():
        fetch_fac(4)

    pl.semaphore_wait(bar, 23)
    swap_t = remote(tpart.at[1 - core], tin, pair_send.at[5], pair_recv.at[5], partner)

    @pl.when(r == 0)
    def _():
        swap_t.start()

    pair = [
        remote(src, dst, pair_send.at[i], pair_recv.at[i], partner)
        for i, (src, dst) in enumerate(
            (
                (dinv.at[0], dv.at[0, mine, :]),
                (fac.at[0, :, first_rows], fv.at[0, mine, first_rows]),
                (dinv.at[pl.ds(1, 4)], dv.at[pl.ds(1, 4), mine, :]),
                (fac.at[pl.ds(1, 3)], fv.at[pl.ds(1, 3), mine, :]),
                (fac.at[0, :, pl.ds(0, 1024)], fv.at[0, mine, pl.ds(0, 1024)]),
            )
        )
    ]
    for cp in pair[:2]:
        cp.start()
        sent.append(cp)

    @pl.when(r == 1)
    def _():
        send_fac(2)
        send_jac(2)
        send_fac(3)
        send_jac(3)

    @pl.when(r == 2)
    def _():
        send_fac(4)
        send_jac(4)

    @pl.when(r != 0)
    def _():
        for cp in load_0:
            cp.wait()

    half = subl(core, 96)
    quarter = subl(h, 48)

    def first_copy(d):
        to = (r + d) % 16
        tx = to // 4
        ty = to % 4
        th = ty // 2
        tg = tx * 2 + (ty + th) % 2
        rows = pl.ds(pl.multiple_of(th * 48, 48), 48)
        t1_cp = remote(t1.at[tg, rows], ts.at[1], own_send.at[0, 0, d], own_recv.at[0, 0], rdev(d))
        x0_cp = remote(x0.at[rows], xf.at[0, rows], own_send.at[0, 1, d], own_recv.at[0, 1], rdev(d))
        return t1_cp, x0_cp

    @pl.when(r == 0)
    def _():
        swap_t.wait_recv()
        for i in range(8):
            t1[i] = tpart[core, i] + tin[i]
        for d in FAR:
            first_copy(d)[0].start()
        ts[1] = t1[0, 0:48]
        pair[0].wait_recv()
        x0[...] = dot3(jt[half, 0:1024], dv[0], NT)
        for d in FAR:
            first_copy(d)[1].start()
        xf[0, 0:48] = x0[0:48]

    @pl.when(r != 0)
    def _():
        pair[0].wait_recv()

    for cp in pair[2:]:
        cp.start()
        sent.append(cp)
    for cp in (load_d, load_f, load_g):
        cp.start()
    def spread_copy(d, b):
        rows = lanes(b * 8 + (z + d) % 8)
        if d == 0:
            return pltpu.make_async_copy(fac.at[4, :, rows], g4.at[core, z, b], z_recv.at[0, b])
        return remote(fac.at[4, :, rows], g4.at[core, z, b], z_send.at[d, b], z_recv.at[d, b], zdev(d))

    def start_spread():
        @pl.when(r >= 2)
        def _():
            for d in (4, 3, 5, 2, 6, 1, 7, 0):
                for b in range(2):
                    spread_copy(d, b).start()

    start_spread()
    for cp in load_j:
        cp.wait()

    @pl.when(r != 0)
    def _():
        pltpu.make_async_copy(ts.at[1], ts.at[1], own_recv.at[0, 0]).wait()

    def forward(j):
        wait_fac(j)
        cp = remote(lts[j].at[:, mine, :], lts[j].at[:, mine, :], fwd_send.at[j], fwd_recv.at[j], partner)
        cp.start()
        sent.append(cp)
        return cp

    fwd = {}
    swap = {}

    def spread_pair():
        return remote(g4.at[core], g4.at[core], z_send.at[0, 0], z_recv.at[8, 0], partner)

    def spread_on():
        @pl.when(r >= 2)
        def _():
            for d in range(8):
                for b in range(2):
                    if d:
                        spread_copy(d, b).wait_recv()
                    else:
                        spread_copy(d, b).wait()
            spread_pair().start()

    paths = ((0, -1, 4), (1, 1, 4), (0, 1, 3), (1, -1, 3))

    def ring_copy(i, s):
        b, way, hops = paths[i]
        return remote(rsend.at[i, s], rbuf.at[i, s], r_send.at[i, s], r_recv.at[i, s], zdev(way))

    def ring(s):
        @pl.when(r >= 2)
        def _():
            for i, (b, way, hops) in enumerate(paths):
                if s >= hops:
                    continue
                target = (z + way * (hops - s) + 8) % 8
                value = u[b, target]
                if s > 0:
                    ring_copy(i, s - 1).wait_recv()
                    value = value + rbuf[i, s - 1]
                rsend[i, s] = value
                ring_copy(i, s).start()

    def exchange(j):
        cp = remote(xf.at[j, quarter, :], xf.at[j, quarter, :], h_send.at[j], h_recv.at[j], hdev)
        cp.start()
        sent.append(cp)
        swap[j] = cp

    def update(j):
        swap[j].wait_recv()
        if j == 0:
            for cp in (load_f, load_g):
                cp.wait()
            for cp in (pair[1], pair[3], pair[4]):
                cp.wait_recv()
        for b in range(2):
            part = dot3(xf[j], fv[j, :, b * 1024:(b + 1) * 1024], NN)
            for i in range(8):
                piece = part[:, i * 128:(i + 1) * 128]
                u[b, i] = piece if j == 0 else u[b, i] + piece

    for j in range(1, 5):
        stage = []
        for d in (4, 3, 5, 2, 6, 1, 7):
            cp = remote(ts.at[j], pa.at[j - 1, d - 1], a_send.at[j - 1, d], a_recv.at[j - 1, d], zdev(d))
            cp.start()
            stage.append(cp)
        sent.extend(stage)
        if j == 1:
            fwd[2] = forward(2)

            @pl.when(r != 0)
            def _():
                pltpu.make_async_copy(xf.at[0, quarter], xf.at[0, quarter], own_recv.at[0, 1]).wait()

            exchange(0)
        if j == 2:
            fwd[4] = forward(4)
            update(0)
        if j > 1:
            update(j - 1)
        if j == 3:
            spread_on()
        if j == 4:
            ring(0)
        for cp in stage:
            cp.wait_recv()
        total = ts[j]
        for d in range(7):
            total = total + pa[j - 1, d]
        rest = -total
        ss[j - 1] = rest
        sb[j - 1, g] = rest
        stage = []
        for dx in (2, 1, 3, 0):
            for dy in (1, 0):
                if dx == 0 and dy == 0:
                    continue
                ny = h * 2 + (y + dy) % 2
                to = {"rows": ((x + dx) % 4) * 4 + ny}
                k = dx * 2 + dy
                cp = remote(ss.at[j - 1], sb.at[j - 1, g], b_send.at[j - 1, k], b_recv.at[j - 1, k], to)
                cp.start()
                stage.append(cp)
        sent.extend(stage)
        if j == 1:
            fwd[3] = forward(3)
        if j == 4:
            ring(1)
        if j < 4:
            fwd[j + 1].wait_recv()
            part = dot3(xf[0, quarter, :], lts[j + 1][0], NN)
            for m in range(1, j):
                part = part + dot3(xf[m, quarter, :], lts[j + 1][m], NN)
            tp[...] = part
        if j == 1:
            load_d.wait()
            pair[2].wait_recv()
        for cp in stage:
            cp.wait_recv()
        new = dot3(jnp.concatenate([sb[j - 1, i] for i in range(8)], axis=1), dv[j], NT)
        if j == 4:
            break
        xf[j, quarter, :] = new
        if j < 4:
            ts[j + 1] = tp[...] + dot3(new, lts[j + 1][j], NN)
            wait_jac(j + 1)

            @pl.when(z < 6)
            def _():
                ts[j + 1, subl(z, 8)] = ts[j + 1, subl(z, 8)] - jtile[j + 1]
        exchange(j)

    xz[h, z] = new

    def pass_on(i, k):
        cp = remote(xz.at[h, i], xz.at[h, i], x_send.at[k], x_recv.at[k], hdev)
        cp.start()
        sent.append(cp)
        return cp

    stage = {}
    for d in (4, 3, 5, 2, 6, 1, 7):
        cp = remote(xz.at[h, z], xz.at[h, z], x_send.at[8 + d], x_recv.at[8 + d], zdev(d))
        cp.start()
        sent.append(cp)
        stage[d] = cp
    passed = [pass_on(z, 0)]
    ring(2)
    for d in (1, 7, 2, 6, 3, 5, 4):
        stage[d].wait_recv()
        passed.append(pass_on((z - d + 8) % 8, d))
    ring(3)

    @pl.when(r >= 2)
    def _():
        spread_pair().wait_recv()

    for cp in passed:
        cp.wait_recv()
    xf[4] = jnp.concatenate([xz[0, z], xz[1, z]], axis=0)
    left = jnp.concatenate([jnp.concatenate([xz[k, i] for i in range(8)], axis=1) for k in range(2)], axis=0)
    right = jnp.concatenate(
        [jnp.concatenate([g4[k, i, b] for i in range(8) for k in range(2)], axis=0) for b in range(2)], axis=1
    )
    tail = dot3(left, right, NN)

    def piece(b, origin):
        return og.at[b * 8 + origin]

    gather = {}

    def hop(i, s):
        b, way, hops = gpaths[i]
        origin = (z - way * s + 8) % 8
        cp = remote(piece(b, origin), piece(b, origin), g_send.at[i, s], g_recv.at[i, s], zdev(way))
        cp.start()
        sent.append(cp)
        gather[i] = cp

    gpaths = ((0, 1, 4), (1, -1, 4), (0, -1, 3), (1, 1, 3))

    @pl.when(r >= 2)
    def _():
        for i, (b, way, hops) in enumerate(paths):
            ring_copy(i, hops - 1).wait_recv()

    for b in range(2):
        first, second = [i for i in range(4) if paths[i][0] == b]
        total = tail[:, b * 128:(b + 1) * 128] + u[b, z] + rbuf[first, paths[first][2] - 1] + rbuf[second, paths[second][2] - 1]
        block = r * 2 + b
        solved = xf[jnp.minimum(block, 4)]
        updated = js[b] - total
        og[b * 8 + z] = jnp.where(block < 5, solved, updated)
        for i in range(4):
            if gpaths[i][0] == b:
                hop(i, 0)
    done = [(0, z), (1, z)]
    shared = []

    def share():
        while done:
            b, origin = done.pop()
            p = b * 8 + origin
            k = len(shared)
            cp = remote(og.at[p], out.at[p, half], o_send.at[k], o_recv.at[k], partner)
            cp.start()
            sent.append(cp)
            shared.append(cp)

    for s in range(1, 5):
        for i in range(4):
            b, way, hops = gpaths[i]
            if s > hops:
                continue
            gather[i].wait_recv()
            if s < hops:
                hop(i, s)
            done.append((b, (z - way * s + 8) % 8))
        if s >= 3:
            share()
    keep = pltpu.make_async_copy(og, out.at[:, half], load_sem.at[8])
    keep.start()
    keep.wait()
    for cp in shared:
        cp.wait_recv()
    for cp in sent:
        cp.wait_send()

    @pl.when(r >= 2)
    def _():
        for d in range(1, 8):
            for b in range(2):
                spread_copy(d, b).wait_send()
        spread_pair().wait_send()
        for i, (b, way, hops) in enumerate(paths):
            for s in range(hops):
                ring_copy(i, s).wait_send()

    @pl.when(r == 0)
    def _():
        swap_t.wait_send()
        for d in range(1, 16):
            for cp in first_copy(d):
                cp.wait_send()

    @pl.when(r == 1)
    def _():
        wait_owner_sends(2)
        wait_owner_sends(3)

    @pl.when(r == 2)
    def _():
        wait_owner_sends(4)

    for j in (2, 3, 4):
        @pl.when(h == owner_h[j])
        def _():
            fac_pass(j).wait_send()


def per_device(jacobian, factor_cols, diag_inverse):
    f32 = jnp.float32
    dma = pltpu.SemaphoreType.DMA
    out = pl.pallas_call(
        kernel,
        out_shape=jax.ShapeDtypeStruct((16, 192, 128), f32),
        in_specs=[pl.BlockSpec(memory_space=pltpu.HBM)] * 3,
        out_specs=pl.BlockSpec(memory_space=pltpu.HBM),
        scratch_shapes=[
            pltpu.VMEM((5, 128, 1024), f32),
            pltpu.VMEM((4, 128, 2048), f32),
            pltpu.VMEM((192, 2048), f32),
            pltpu.VMEM((2, 96, 128), f32),
            pltpu.VMEM((96, 128), f32),
            pltpu.VMEM((8, 96, 128), f32),
            pltpu.VMEM((2, 8, 96, 128), f32),
            pltpu.VMEM((8, 96, 128), f32),
            pltpu.VMEM((6, 8, 64, 128), f32),
            pltpu.VMEM((5, 48, 128), f32),
            pltpu.VMEM((48, 128), f32),
            pltpu.VMEM((5, 96, 128), f32),
            pltpu.VMEM((2, 128, 128), f32),
            pltpu.VMEM((3, 128, 128), f32),
            pltpu.VMEM((4, 128, 128), f32),
            pltpu.VMEM((5, 8, 128), f32),
            pltpu.VMEM((4, 7, 48, 128), f32),
            pltpu.VMEM((4, 48, 128), f32),
            pltpu.VMEM((4, 8, 48, 128), f32),
            pltpu.VMEM((2, 8, 96, 128), f32),
            pltpu.VMEM((4, 4, 96, 128), f32),
            pltpu.VMEM((4, 4, 96, 128), f32),
            pltpu.VMEM((16, 96, 128), f32),
            pltpu.VMEM((2, 8, 2, 64, 128), f32),
            pltpu.VMEM((2, 8, 48, 128), f32),
            dma((9,)),
            dma((6,)), dma((6,)),
            dma((5, 2, 16)), dma((5, 2)),
            dma((5,)), dma((5,)),
            dma((5,)), dma((5,)),
            dma((4, 8)), dma((4, 8)),
            dma((4, 8)), dma((4, 8)),
            dma((5,)), dma((5,)),
            dma((4, 4)), dma((4, 4)),
            dma((4, 4)), dma((4, 4)),
            dma((16,)), dma((16,)),
            dma((8, 2)), dma((9, 2)),
            dma((16,)), dma((16,)),
        ],
        compiler_params=pltpu.CompilerParams(
            collective_id=0, has_side_effects=True, vmem_limit_bytes=57 * 1024 * 1024
        ),
        name="whiten",
    )(jacobian.T, factor_cols, diag_inverse)
    return jnp.transpose(out, (0, 2, 1)).reshape(2048, 192)


def solution(mesh):
    in_specs = (P("rows", None), P(None, "cols", "rows"), P(None, "cols", None))
    return jax.shard_map(
        per_device, mesh=mesh, in_specs=in_specs, out_specs=P("rows", None), check_vma=False
    )
```

```python
import jax
import jax.numpy as jnp
from jax import lax
from jax.experimental import pallas as pl
from jax.experimental.pallas import tpu as pltpu
from jax.sharding import PartitionSpec as P

MESH = pl.DeviceIdType.MESH
FAR = (10, 8, 9, 11, 6, 5, 7, 4, 14, 13, 15, 12, 2, 1, 3)
NT = (((1,), (1,)), ((), ()))
NN = (((1,), (0,)), ((), ()))


def halves(a):
    hi = a.astype(jnp.bfloat16)
    lo = (a - hi.astype(jnp.float32)).astype(jnp.bfloat16)
    return hi, lo


def dot3(a, b, dims):
    ah, al = halves(a)
    bh, bl = halves(b)

    def one(p, q):
        return lax.dot_general(p, q, dims, preferred_element_type=jnp.float32)

    return one(ah, bh) + (one(ah, bl) + one(al, bh))


def dot3_split(a, bh, bl, dims):
    ah, al = halves(a)

    def one(p, q):
        return lax.dot_general(p, q, dims, preferred_element_type=jnp.float32)

    return one(ah, bh) + (one(ah, bl) + one(al, bh))


def lanes(i, n=128):
    return pl.ds(pl.multiple_of(i * n, n), n)


def subl(i, n):
    return pl.ds(pl.multiple_of(i * n, n), n)


def kernel(
    jac, fac, dinv, out,
    dv, fv, jt, js, x0, t1, tpart, tin, stage_f, ts, tp, xf, lt2, lt3, lt4, jtile,
    pa, ss, sb, u, rsend, rbuf, og, g4, xz, dsplit,
    load_sem, pair_send, pair_recv, own_send, own_recv, fwd_send, fwd_recv, pass_send, pass_recv,
    a_send, a_recv, b_send, b_recv, h_send, h_recv, r_send, r_recv, g_send, g_recv, o_send, o_recv, z_send, z_recv, x_send, x_recv,
):
    r = lax.axis_index("rows")
    c = lax.axis_index("cols")
    x = r // 4
    y = r % 4
    z = c // 2
    core = c % 2
    h = y // 2
    g = x * 2 + (y + h) % 2

    def zdev(d):
        return {"cols": ((z + d + 8) % 8) * 2 + core}

    def rdev(d):
        return {"rows": (r + d) % 16}

    partner = {"cols": c + 1 - 2 * core}
    hdev = {"rows": x * 4 + 3 - y}

    def remote(src, dst, ssem, rsem, dev):
        return pltpu.make_async_remote_copy(
            src_ref=src, dst_ref=dst, send_sem=ssem, recv_sem=rsem, device_id=dev, device_id_type=MESH
        )

    sent = []

    bar = pltpu.get_barrier_semaphore()
    for d in range(1, 16):
        pl.semaphore_signal(bar, inc=1, device_id=rdev(d), device_id_type=MESH)
    for d in range(1, 8):
        pl.semaphore_signal(bar, inc=1, device_id=zdev(d), device_id_type=MESH)
    pl.semaphore_signal(bar, inc=1, device_id=partner, device_id_type=MESH)

    mine = subl(core, 64)
    first_rows = pl.ds(1024, 1024)
    load_0 = [
        pltpu.make_async_copy(dinv.at[0], dv.at[0, mine, :], load_sem.at[0]),
        pltpu.make_async_copy(fac.at[0, :, first_rows], fv.at[0, mine, first_rows], load_sem.at[1]),
    ]
    load_d = pltpu.make_async_copy(dinv.at[pl.ds(1, 4)], dv.at[pl.ds(1, 4), mine, :], load_sem.at[5])
    load_f = pltpu.make_async_copy(fac.at[pl.ds(1, 3)], fv.at[pl.ds(1, 3), mine, :], load_sem.at[6])
    load_g = pltpu.make_async_copy(fac.at[0, :, pl.ds(0, 1024)], fv.at[0, mine, pl.ds(0, 1024)], load_sem.at[7])
    for cp in load_0:
        cp.start()
    load_j = [
        pltpu.make_async_copy(
            jac.at[subl(core, 96), pl.ds(pl.multiple_of(b * 1024 + z * 128, 128), 128)], js.at[b], load_sem.at[2 + b]
        )
        for b in range(2)
    ]
    for cp in load_j:
        cp.start()

    load_jt = pltpu.make_async_copy(jac, jt, load_sem.at[4])

    @pl.when(r == 0)
    def _():
        load_jt.start()
        for cp in load_0:
            cp.wait()
        load_jt.wait()
        first = dot3(jt[:, 0:1024], dv[0, mine, :], NT)
        whole = dot3(first, fv[0, mine, 1024:2048], NN)
        for i in range(8):
            for k in range(2):
                tpart[k, i] = whole[k * 96:(k + 1) * 96, i * 128:(i + 1) * 128]

        @pl.when(c == 0)
        def _():
            for i in range(8):
                for k in range(2):
                    tpart[k, i] = tpart[k, i] - jt[k * 96:(k + 1) * 96, 1024 + i * 128:1024 + (i + 1) * 128]

    lts = {2: lt2, 3: lt3, 4: lt4}
    owner_h = {2: 0, 3: 0, 4: 1}

    def fac_copy(j, k, fetch=False):
        tx = (x + k // 2) % 4
        ty = h * 2 + (y % 2 + k % 2) % 2
        tg = tx * 2 + (ty + h) % 2
        rows = pl.ds(pl.multiple_of((j % 2) * 1024 + tg * 128, 128), 128)
        dst = lts[j].at[:, mine, :]
        part = stage_f.at[pl.ds(0 if j == 4 else 3 * (j - 2), j), k]
        if fetch:
            return pltpu.make_async_copy(fac.at[pl.ds(0, j), :, rows], dst if k == 0 else part, own_send.at[j, 0, k] if k else own_recv.at[j, 0])
        return remote(part, dst, own_send.at[j, 0, k], own_recv.at[j, 0], {"rows": tx * 4 + ty})

    def jac_copy(j, d):
        to = (r + d) % 16
        tx = to // 4
        ty = to % 4
        th = ty // 2
        tg = tx * 2 + (ty + th) % 2
        rows = pl.ds(pl.multiple_of((j % 2) * 1024 + tg * 128, 128), 128)
        src = jac.at[pl.ds(pl.multiple_of(core * 96 + th * 48 + z * 8, 8), 8), rows]
        if d == 0:
            return pltpu.make_async_copy(src, jtile.at[j], own_recv.at[j, 1])
        return remote(src, jtile.at[j], own_send.at[j, 1, d], own_recv.at[j, 1], rdev(d))

    def fetch_fac(j):
        for k in (4, 5, 2, 3, 6, 7, 1, 0):
            fac_copy(j, k, True).start()

    def send_fac(j):
        for k in (4, 5, 2, 3, 6, 7, 1):
            fac_copy(j, k, True).wait()
            fac_copy(j, k).start()

    def send_jac(j):
        @pl.when(z < 6)
        def _():
            for d in range(16):
                jac_copy(j, d).start()

    def wait_fac(j):
        @pl.when(h == owner_h[j])
        def _():
            pltpu.make_async_copy(lts[j].at[:, mine, :], lts[j].at[:, mine, :], own_recv.at[j, 0]).wait()
            fac_pass(j).start()

        @pl.when(h != owner_h[j])
        def _():
            fac_pass(j).wait_recv()

    def fac_pass(j):
        return remote(lts[j].at[:, mine, :], lts[j].at[:, mine, :], pass_send.at[j], pass_recv.at[j], hdev)

    def wait_jac(j):
        @pl.when(z < 6)
        def _():
            pltpu.make_async_copy(jtile.at[j], jtile.at[j], own_recv.at[j, 1]).wait()

    def wait_owner_sends(j):
        for k in range(1, 8):
            fac_copy(j, k).wait_send()

        @pl.when(z < 6)
        def _():
            for d in range(1, 16):
                jac_copy(j, d).wait_send()

    @pl.when(r == 1)
    def _():
        fetch_fac(2)
        fetch_fac(3)

    @pl.when(r == 2)
    def _():
        fetch_fac(4)

    pl.semaphore_wait(bar, 23)
    swap_t = remote(tpart.at[1 - core], tin, pair_send.at[5], pair_recv.at[5], partner)

    @pl.when(r == 0)
    def _():
        swap_t.start()

    pair = [
        remote(src, dst, pair_send.at[i], pair_recv.at[i], partner)
        for i, (src, dst) in enumerate(
            (
                (dinv.at[0], dv.at[0, mine, :]),
                (fac.at[0, :, first_rows], fv.at[0, mine, first_rows]),
                (dinv.at[pl.ds(1, 4)], dv.at[pl.ds(1, 4), mine, :]),
                (fac.at[pl.ds(1, 3)], fv.at[pl.ds(1, 3), mine, :]),
                (fac.at[0, :, pl.ds(0, 1024)], fv.at[0, mine, pl.ds(0, 1024)]),
            )
        )
    ]

    @pl.when(r == 0)
    def _():
        pair[0].start()

    @pl.when(r == 1)
    def _():
        send_fac(2)
        send_jac(2)
        send_fac(3)
        send_jac(3)

    @pl.when(r == 2)
    def _():
        send_fac(4)
        send_jac(4)

    @pl.when(r != 0)
    def _():
        for cp in load_0:
            cp.wait()

    half = subl(core, 96)
    quarter = subl(h, 48)

    def first_copy(d):
        to = (r + d) % 16
        tx = to // 4
        ty = to % 4
        th = ty // 2
        tg = tx * 2 + (ty + th) % 2
        rows = pl.ds(pl.multiple_of(th * 48, 48), 48)
        t1_cp = remote(t1.at[tg, rows], ts.at[1], own_send.at[0, 0, d], own_recv.at[0, 0], rdev(d))
        x0_cp = remote(x0.at[rows], xf.at[0, rows], own_send.at[0, 1, d], own_recv.at[0, 1], rdev(d))
        return t1_cp, x0_cp

    @pl.when(r == 0)
    def _():
        swap_t.wait_recv()
        for i in range(8):
            t1[i] = tpart[core, i] + tin[i]
        for d in FAR:
            first_copy(d)[0].start()
        ts[1] = t1[0, 0:48]
        pair[0].wait_recv()
        x0[...] = dot3(jt[half, 0:1024], dv[0], NT)
        for d in FAR:
            first_copy(d)[1].start()
        xf[0, 0:48] = x0[0:48]

    def spread_copy(d, b):
        rows = lanes(b * 8 + (z + d) % 8)
        if d == 0:
            return pltpu.make_async_copy(fac.at[4, :, rows], g4.at[core, z, b], z_recv.at[0, b])
        return remote(fac.at[4, :, rows], g4.at[core, z, b], z_send.at[d, b], z_recv.at[d, b], zdev(d))

    def start_spread():
        @pl.when(r >= 2)
        def _():
            for d in (4, 3, 5, 2, 6, 1, 7, 0):
                for b in range(2):
                    spread_copy(d, b).start()

    start_spread()
    pair[2].start()
    sent.append(pair[2])
    load_d.start()
    for cp in load_j:
        cp.wait()

    @pl.when(r != 0)
    def _():
        pltpu.make_async_copy(ts.at[1], ts.at[1], own_recv.at[0, 0]).wait()

    def forward(j):
        wait_fac(j)
        cp = remote(lts[j].at[:, mine, :], lts[j].at[:, mine, :], fwd_send.at[j], fwd_recv.at[j], partner)
        cp.start()
        sent.append(cp)
        return cp

    fwd = {}
    swap = {}

    def spread_pair():
        return remote(g4.at[core], g4.at[core], z_send.at[0, 0], z_recv.at[8, 0], partner)

    def spread_on():
        @pl.when(r >= 2)
        def _():
            for d in range(8):
                for b in range(2):
                    if d:
                        spread_copy(d, b).wait_recv()
                    else:
                        spread_copy(d, b).wait()
            spread_pair().start()

    paths = ((0, -1, 4), (1, 1, 4), (0, 1, 3), (1, -1, 3))

    def ring_copy(i, s):
        b, way, hops = paths[i]
        return remote(rsend.at[i, s], rbuf.at[i, s], r_send.at[i, s], r_recv.at[i, s], zdev(way))

    def ring(s):
        @pl.when(r >= 2)
        def _():
            for i, (b, way, hops) in enumerate(paths):
                if s >= hops:
                    continue
                target = (z + way * (hops - s) + 8) % 8
                value = u[b, target]
                if s > 0:
                    ring_copy(i, s - 1).wait_recv()
                    value = value + rbuf[i, s - 1]
                rsend[i, s] = value
                ring_copy(i, s).start()

    def exchange(j):
        cp = remote(xf.at[j, quarter, :], xf.at[j, quarter, :], h_send.at[j], h_recv.at[j], hdev)
        cp.start()
        sent.append(cp)
        swap[j] = cp

    def update(j):
        swap[j].wait_recv()
        if j == 0:
            for cp in (load_f, load_g):
                cp.wait()
            for cp in (pair[1], pair[3], pair[4]):
                cp.wait_recv()
        for b in range(2):
            part = dot3(xf[j], fv[j, :, b * 1024:(b + 1) * 1024], NN)
            for i in range(8):
                piece = part[:, i * 128:(i + 1) * 128]
                u[b, i] = piece if j == 0 else u[b, i] + piece

    for j in range(1, 5):
        stage = []
        for d in (4, 3, 5, 2, 6, 1, 7):
            cp = remote(ts.at[j], pa.at[j - 1, d - 1], a_send.at[j - 1, d], a_recv.at[j - 1, d], zdev(d))
            cp.start()
            stage.append(cp)
        sent.extend(stage)
        if j == 1:
            for cp in (pair[1], pair[3], pair[4]):
                cp.start()
                sent.append(cp)
            load_f.start()
            load_g.start()
            fwd[2] = forward(2)

            @pl.when(r != 0)
            def _():
                pltpu.make_async_copy(xf.at[0, quarter], xf.at[0, quarter], own_recv.at[0, 1]).wait()

            exchange(0)
            load_d.wait()
            pair[2].wait_recv()
        elif j < 4:
            fwd[j + 1] = forward(j + 1)
            update(j - 2)
        else:
            update(2)
            spread_on()
            update(3)
            ring(0)
        hi, lo = halves(dv[j])
        dsplit[0] = hi
        dsplit[1] = lo
        for cp in stage:
            cp.wait_recv()
        total = ts[j]
        for d in range(7):
            total = total + pa[j - 1, d]
        rest = -total
        ss[j - 1] = rest
        sb[j - 1, g] = rest
        stage = []
        for dx in (2, 1, 3, 0):
            for dy in (1, 0):
                if dx == 0 and dy == 0:
                    continue
                ny = h * 2 + (y + dy) % 2
                to = {"rows": ((x + dx) % 4) * 4 + ny}
                k = dx * 2 + dy
                cp = remote(ss.at[j - 1], sb.at[j - 1, g], b_send.at[j - 1, k], b_recv.at[j - 1, k], to)
                cp.start()
                stage.append(cp)
        sent.extend(stage)
        if j == 4:
            ring(1)
        if j < 4:
            fwd[j + 1].wait_recv()
            part = dot3(xf[0, quarter, :], lts[j + 1][0], NN)
            for m in range(1, j):
                part = part + dot3(xf[m, quarter, :], lts[j + 1][m], NN)
            tp[...] = part
        for cp in stage:
            cp.wait_recv()
        rows = jnp.concatenate([sb[j - 1, i] for i in range(8)], axis=1)
        new = dot3_split(rows, dsplit[0], dsplit[1], NT)
        if j == 4:
            break
        xf[j, quarter, :] = new
        if j < 4:
            ts[j + 1] = tp[...] + dot3(new, lts[j + 1][j], NN)
            wait_jac(j + 1)

            @pl.when(z < 6)
            def _():
                ts[j + 1, subl(z, 8)] = ts[j + 1, subl(z, 8)] - jtile[j + 1]
        exchange(j)

    xz[h, z] = new

    def pass_on(i, k):
        cp = remote(xz.at[h, i], xz.at[h, i], x_send.at[k], x_recv.at[k], hdev)
        cp.start()
        sent.append(cp)
        return cp

    stage = {}
    for d in (4, 3, 5, 2, 6, 1, 7):
        cp = remote(xz.at[h, z], xz.at[h, z], x_send.at[8 + d], x_recv.at[8 + d], zdev(d))
        cp.start()
        sent.append(cp)
        stage[d] = cp
    passed = [pass_on(z, 0)]
    ring(2)
    for d in (1, 7, 2, 6, 3, 5, 4):
        stage[d].wait_recv()
        passed.append(pass_on((z - d + 8) % 8, d))
    ring(3)

    @pl.when(r >= 2)
    def _():
        spread_pair().wait_recv()

    right = jnp.concatenate(
        [jnp.concatenate([g4[k, i, b] for i in range(8) for k in range(2)], axis=0) for b in range(2)], axis=1
    )
    right_hi, right_lo = halves(right)
    for cp in passed:
        cp.wait_recv()
    xf[4] = jnp.concatenate([xz[0, z], xz[1, z]], axis=0)
    left = jnp.concatenate([jnp.concatenate([xz[k, i] for i in range(8)], axis=1) for k in range(2)], axis=0)
    tail = dot3_split(left, right_hi, right_lo, NN)

    def piece(b, origin):
        return og.at[b * 8 + origin]

    gather = {}

    def hop(i, s):
        b, way, hops = gpaths[i]
        origin = (z - way * s + 8) % 8
        cp = remote(piece(b, origin), piece(b, origin), g_send.at[i, s], g_recv.at[i, s], zdev(way))
        cp.start()
        sent.append(cp)
        gather[i] = cp

    gpaths = ((0, 1, 4), (1, -1, 4), (0, -1, 3), (1, 1, 3))

    @pl.when(r >= 2)
    def _():
        for i, (b, way, hops) in enumerate(paths):
            ring_copy(i, hops - 1).wait_recv()

    for b in range(2):
        first, second = [i for i in range(4) if paths[i][0] == b]
        total = tail[:, b * 128:(b + 1) * 128] + u[b, z] + rbuf[first, paths[first][2] - 1] + rbuf[second, paths[second][2] - 1]
        block = r * 2 + b
        solved = xf[jnp.minimum(block, 4)]
        updated = js[b] - total
        og[b * 8 + z] = jnp.where(block < 5, solved, updated)
        for i in range(4):
            if gpaths[i][0] == b:
                hop(i, 0)
    done = [(0, z), (1, z)]
    shared = []

    def share():
        while done:
            b, origin = done.pop()
            p = b * 8 + origin
            k = len(shared)
            cp = remote(og.at[p], out.at[p, half], o_send.at[k], o_recv.at[k], partner)
            cp.start()
            sent.append(cp)
            shared.append(cp)

    for s in range(1, 5):
        for i in range(4):
            b, way, hops = gpaths[i]
            if s > hops:
                continue
            gather[i].wait_recv()
            if s < hops:
                hop(i, s)
            done.append((b, (z - way * s + 8) % 8))
        if s >= 3:
            share()
    keep = pltpu.make_async_copy(og, out.at[:, half], load_sem.at[8])
    keep.start()
    keep.wait()
    for cp in shared:
        cp.wait_recv()
    for cp in sent:
        cp.wait_send()

    @pl.when(r >= 2)
    def _():
        for d in range(1, 8):
            for b in range(2):
                spread_copy(d, b).wait_send()
        spread_pair().wait_send()
        for i, (b, way, hops) in enumerate(paths):
            for s in range(hops):
                ring_copy(i, s).wait_send()

    @pl.when(r == 0)
    def _():
        swap_t.wait_send()
        pair[0].wait_send()
        for d in range(1, 16):
            for cp in first_copy(d):
                cp.wait_send()

    @pl.when(r == 1)
    def _():
        wait_owner_sends(2)
        wait_owner_sends(3)

    @pl.when(r == 2)
    def _():
        wait_owner_sends(4)

    for j in (2, 3, 4):
        @pl.when(h == owner_h[j])
        def _():
            fac_pass(j).wait_send()


def per_device(jacobian, factor_cols, diag_inverse):
    f32 = jnp.float32
    dma = pltpu.SemaphoreType.DMA
    out = pl.pallas_call(
        kernel,
        out_shape=jax.ShapeDtypeStruct((16, 192, 128), f32),
        in_specs=[pl.BlockSpec(memory_space=pltpu.HBM)] * 3,
        out_specs=pl.BlockSpec(memory_space=pltpu.HBM),
        scratch_shapes=[
            pltpu.VMEM((5, 128, 1024), f32),
            pltpu.VMEM((4, 128, 2048), f32),
            pltpu.VMEM((192, 2048), f32),
            pltpu.VMEM((2, 96, 128), f32),
            pltpu.VMEM((96, 128), f32),
            pltpu.VMEM((8, 96, 128), f32),
            pltpu.VMEM((2, 8, 96, 128), f32),
            pltpu.VMEM((8, 96, 128), f32),
            pltpu.VMEM((6, 8, 64, 128), f32),
            pltpu.VMEM((5, 48, 128), f32),
            pltpu.VMEM((48, 128), f32),
            pltpu.VMEM((5, 96, 128), f32),
            pltpu.VMEM((2, 128, 128), f32),
            pltpu.VMEM((3, 128, 128), f32),
            pltpu.VMEM((4, 128, 128), f32),
            pltpu.VMEM((5, 8, 128), f32),
            pltpu.VMEM((4, 7, 48, 128), f32),
            pltpu.VMEM((4, 48, 128), f32),
            pltpu.VMEM((4, 8, 48, 128), f32),
            pltpu.VMEM((2, 8, 96, 128), f32),
            pltpu.VMEM((4, 4, 96, 128), f32),
            pltpu.VMEM((4, 4, 96, 128), f32),
            pltpu.VMEM((16, 96, 128), f32),
            pltpu.VMEM((2, 8, 2, 64, 128), f32),
            pltpu.VMEM((2, 8, 48, 128), f32),
            pltpu.VMEM((2, 128, 1024), jnp.bfloat16),
            dma((9,)),
            dma((6,)), dma((6,)),
            dma((5, 2, 16)), dma((5, 2)),
            dma((5,)), dma((5,)),
            dma((5,)), dma((5,)),
            dma((4, 8)), dma((4, 8)),
            dma((4, 8)), dma((4, 8)),
            dma((5,)), dma((5,)),
            dma((4, 4)), dma((4, 4)),
            dma((4, 4)), dma((4, 4)),
            dma((16,)), dma((16,)),
            dma((8, 2)), dma((9, 2)),
            dma((16,)), dma((16,)),
        ],
        compiler_params=pltpu.CompilerParams(
            collective_id=0, has_side_effects=True, vmem_limit_bytes=57 * 1024 * 1024
        ),
        name="whiten",
    )(jacobian.T, factor_cols, diag_inverse)
    return jnp.transpose(out, (0, 2, 1)).reshape(2048, 192)


def solution(mesh):
    in_specs = (P("rows", None), P(None, "cols", "rows"), P(None, "cols", None))
    return jax.shard_map(
        per_device, mesh=mesh, in_specs=in_specs, out_specs=P("rows", None), check_vma=False
    )
```

```python
import jax
import jax.numpy as jnp
from jax import lax
from jax.experimental import pallas as pl
from jax.experimental.pallas import tpu as pltpu
from jax.sharding import PartitionSpec as P

MESH = pl.DeviceIdType.MESH
FAR = (10, 8, 9, 11, 6, 5, 7, 4, 14, 13, 15, 12, 2, 1, 3)
NT = (((1,), (1,)), ((), ()))
NN = (((1,), (0,)), ((), ()))


def halves(a):
    hi = a.astype(jnp.bfloat16)
    lo = (a - hi.astype(jnp.float32)).astype(jnp.bfloat16)
    return hi, lo


def dot3(a, b, dims):
    ah, al = halves(a)
    bh, bl = halves(b)

    def one(p, q):
        return lax.dot_general(p, q, dims, preferred_element_type=jnp.float32)

    return one(ah, bh) + (one(ah, bl) + one(al, bh))


def dot3_split(a, bh, bl, dims):
    ah, al = halves(a)

    def one(p, q):
        return lax.dot_general(p, q, dims, preferred_element_type=jnp.float32)

    return one(ah, bh) + (one(ah, bl) + one(al, bh))


def lanes(i, n=128):
    return pl.ds(pl.multiple_of(i * n, n), n)


def subl(i, n):
    return pl.ds(pl.multiple_of(i * n, n), n)


def kernel(
    jac, fac, dinv, out,
    dv, fv, jt, js, x0, t1, tpart, tin, stage_f, ts, tp, xf, lt2, lt3, lt4, jtile,
    pa, ss, sb, u, rsend, rbuf, og, g4, xz, dsplit,
    load_sem, pair_send, pair_recv, own_send, own_recv, fwd_send, fwd_recv, pass_send, pass_recv,
    a_send, a_recv, b_send, b_recv, h_send, h_recv, r_send, r_recv, g_send, g_recv, o_send, o_recv, z_send, z_recv, x_send, x_recv,
):
    r = lax.axis_index("rows")
    c = lax.axis_index("cols")
    x = r // 4
    y = r % 4
    z = c // 2
    core = c % 2
    h = y // 2
    g = x * 2 + (y + h) % 2

    def zdev(d):
        return {"cols": ((z + d + 8) % 8) * 2 + core}

    def rdev(d):
        return {"rows": (r + d) % 16}

    partner = {"cols": c + 1 - 2 * core}
    hdev = {"rows": x * 4 + 3 - y}

    def remote(src, dst, ssem, rsem, dev):
        return pltpu.make_async_remote_copy(
            src_ref=src, dst_ref=dst, send_sem=ssem, recv_sem=rsem, device_id=dev, device_id_type=MESH
        )

    sent = []

    bar = pltpu.get_barrier_semaphore()
    for d in range(1, 16):
        pl.semaphore_signal(bar, inc=1, device_id=rdev(d), device_id_type=MESH)
    for d in range(1, 8):
        pl.semaphore_signal(bar, inc=1, device_id=zdev(d), device_id_type=MESH)
    pl.semaphore_signal(bar, inc=1, device_id=partner, device_id_type=MESH)

    mine = subl(core, 64)
    first_rows = pl.ds(1024, 1024)
    load_0 = [
        pltpu.make_async_copy(dinv.at[0], dv.at[0, mine, :], load_sem.at[0]),
        pltpu.make_async_copy(fac.at[0, :, first_rows], fv.at[0, mine, first_rows], load_sem.at[1]),
    ]
    load_d = pltpu.make_async_copy(dinv.at[pl.ds(1, 4)], dv.at[pl.ds(1, 4), mine, :], load_sem.at[5])
    load_f = pltpu.make_async_copy(fac.at[pl.ds(1, 3)], fv.at[pl.ds(1, 3), mine, :], load_sem.at[6])
    load_g = pltpu.make_async_copy(fac.at[0, :, pl.ds(0, 1024)], fv.at[0, mine, pl.ds(0, 1024)], load_sem.at[7])
    for cp in load_0:
        cp.start()
    load_j = [
        pltpu.make_async_copy(
            jac.at[subl(core, 96), pl.ds(pl.multiple_of(b * 1024 + z * 128, 128), 128)], js.at[b], load_sem.at[2 + b]
        )
        for b in range(2)
    ]
    for cp in load_j:
        cp.start()

    load_jt = pltpu.make_async_copy(jac, jt, load_sem.at[4])

    @pl.when(r == 0)
    def _():
        load_jt.start()
        for cp in load_0:
            cp.wait()
        load_jt.wait()
        first = dot3(jt[:, 0:1024], dv[0, mine, :], NT)
        whole = dot3(first, fv[0, mine, 1024:2048], NN)
        for i in range(8):
            for k in range(2):
                tpart[k, i] = whole[k * 96:(k + 1) * 96, i * 128:(i + 1) * 128]

        @pl.when(c == 0)
        def _():
            for i in range(8):
                for k in range(2):
                    tpart[k, i] = tpart[k, i] - jt[k * 96:(k + 1) * 96, 1024 + i * 128:1024 + (i + 1) * 128]

    lts = {2: lt2, 3: lt3, 4: lt4}
    owner_h = {2: 0, 3: 0, 4: 1}

    def fac_copy(j, k, fetch=False):
        tx = (x + k // 2) % 4
        ty = h * 2 + (y % 2 + k % 2) % 2
        tg = tx * 2 + (ty + h) % 2
        rows = pl.ds(pl.multiple_of((j % 2) * 1024 + tg * 128, 128), 128)
        dst = lts[j].at[:, mine, :]
        part = stage_f.at[pl.ds(0 if j == 4 else 3 * (j - 2), j), k]
        if fetch:
            return pltpu.make_async_copy(fac.at[pl.ds(0, j), :, rows], dst if k == 0 else part, own_send.at[j, 0, k] if k else own_recv.at[j, 0])
        return remote(part, dst, own_send.at[j, 0, k], own_recv.at[j, 0], {"rows": tx * 4 + ty})

    def jac_copy(j, d):
        to = (r + d) % 16
        tx = to // 4
        ty = to % 4
        th = ty // 2
        tg = tx * 2 + (ty + th) % 2
        rows = pl.ds(pl.multiple_of((j % 2) * 1024 + tg * 128, 128), 128)
        src = jac.at[pl.ds(pl.multiple_of(core * 96 + th * 48 + z * 8, 8), 8), rows]
        if d == 0:
            return pltpu.make_async_copy(src, jtile.at[j], own_recv.at[j, 1])
        return remote(src, jtile.at[j], own_send.at[j, 1, d], own_recv.at[j, 1], rdev(d))

    def fetch_fac(j):
        for k in (4, 5, 2, 3, 6, 7, 1, 0):
            fac_copy(j, k, True).start()

    def send_fac(j):
        for k in (4, 5, 2, 3, 6, 7, 1):
            fac_copy(j, k, True).wait()
            fac_copy(j, k).start()

    def send_jac(j):
        @pl.when(z < 6)
        def _():
            for d in range(16):
                jac_copy(j, d).start()

    def wait_fac(j):
        @pl.when(h == owner_h[j])
        def _():
            pltpu.make_async_copy(lts[j].at[:, mine, :], lts[j].at[:, mine, :], own_recv.at[j, 0]).wait()
            fac_pass(j).start()

        @pl.when(h != owner_h[j])
        def _():
            fac_pass(j).wait_recv()

    def fac_pass(j):
        return remote(lts[j].at[:, mine, :], lts[j].at[:, mine, :], pass_send.at[j], pass_recv.at[j], hdev)

    def wait_jac(j):
        @pl.when(z < 6)
        def _():
            pltpu.make_async_copy(jtile.at[j], jtile.at[j], own_recv.at[j, 1]).wait()

    def wait_owner_sends(j):
        for k in range(1, 8):
            fac_copy(j, k).wait_send()

        @pl.when(z < 6)
        def _():
            for d in range(1, 16):
                jac_copy(j, d).wait_send()

    @pl.when(r == 1)
    def _():
        fetch_fac(2)
        fetch_fac(3)

    @pl.when(r == 2)
    def _():
        fetch_fac(4)

    pl.semaphore_wait(bar, 23)
    swap_t = remote(tpart.at[1 - core], tin, pair_send.at[5], pair_recv.at[5], partner)

    @pl.when(r == 0)
    def _():
        swap_t.start()

    pair = [
        remote(src, dst, pair_send.at[i], pair_recv.at[i], partner)
        for i, (src, dst) in enumerate(
            (
                (dinv.at[0], dv.at[0, mine, :]),
                (fac.at[0, :, first_rows], fv.at[0, mine, first_rows]),
                (dinv.at[pl.ds(1, 4)], dv.at[pl.ds(1, 4), mine, :]),
                (fac.at[pl.ds(1, 3)], fv.at[pl.ds(1, 3), mine, :]),
                (fac.at[0, :, pl.ds(0, 1024)], fv.at[0, mine, pl.ds(0, 1024)]),
            )
        )
    ]

    @pl.when(r == 0)
    def _():
        pair[0].start()

    @pl.when(r == 1)
    def _():
        send_fac(2)
        send_jac(2)
        send_fac(3)
        send_jac(3)

    @pl.when(r == 2)
    def _():
        send_fac(4)
        send_jac(4)

    @pl.when(r != 0)
    def _():
        for cp in load_0:
            cp.wait()

    half = subl(core, 96)
    quarter = subl(h, 48)

    def first_copy(d):
        to = (r + d) % 16
        tx = to // 4
        ty = to % 4
        th = ty // 2
        tg = tx * 2 + (ty + th) % 2
        rows = pl.ds(pl.multiple_of(th * 48, 48), 48)
        t1_cp = remote(t1.at[tg, rows], ts.at[1], own_send.at[0, 0, d], own_recv.at[0, 0], rdev(d))
        x0_cp = remote(x0.at[rows], xf.at[0, rows], own_send.at[0, 1, d], own_recv.at[0, 1], rdev(d))
        return t1_cp, x0_cp

    @pl.when(r == 0)
    def _():
        swap_t.wait_recv()
        for i in range(8):
            t1[i] = tpart[core, i] + tin[i]
        for d in FAR:
            first_copy(d)[0].start()
        ts[1] = t1[0, 0:48]
        pair[0].wait_recv()
        x0[...] = dot3(jt[half, 0:1024], dv[0], NT)
        for d in FAR:
            first_copy(d)[1].start()
        xf[0, 0:48] = x0[0:48]

    def spread_copy(d, b):
        rows = lanes(b * 8 + (z + d) % 8)
        if d == 0:
            return pltpu.make_async_copy(fac.at[4, :, rows], g4.at[core, z, b], z_recv.at[0, b])
        return remote(fac.at[4, :, rows], g4.at[core, z, b], z_send.at[d, b], z_recv.at[d, b], zdev(d))

    def start_spread():
        @pl.when(r >= 2)
        def _():
            for d in (4, 3, 5, 2, 6, 1, 7, 0):
                for b in range(2):
                    spread_copy(d, b).start()

    start_spread()
    pair[2].start()
    sent.append(pair[2])
    load_d.start()
    for cp in load_j:
        cp.wait()

    @pl.when(r != 0)
    def _():
        pltpu.make_async_copy(ts.at[1], ts.at[1], own_recv.at[0, 0]).wait()

    def forward(j):
        wait_fac(j)
        cp = remote(lts[j].at[:, mine, :], lts[j].at[:, mine, :], fwd_send.at[j], fwd_recv.at[j], partner)
        cp.start()
        sent.append(cp)
        return cp

    fwd = {}
    swap = {}

    def spread_pair():
        return remote(g4.at[core], g4.at[core], z_send.at[0, 0], z_recv.at[8, 0], partner)

    def spread_on():
        @pl.when(r >= 2)
        def _():
            for d in range(8):
                for b in range(2):
                    if d:
                        spread_copy(d, b).wait_recv()
                    else:
                        spread_copy(d, b).wait()
            spread_pair().start()

    paths = ((0, -1, 4), (1, 1, 4), (0, 1, 3), (1, -1, 3))

    def ring_copy(i, s):
        b, way, hops = paths[i]
        return remote(rsend.at[i, s], rbuf.at[i, s], r_send.at[i, s], r_recv.at[i, s], zdev(way))

    def ring(s):
        @pl.when(r >= 2)
        def _():
            for i, (b, way, hops) in enumerate(paths):
                if s >= hops:
                    continue
                target = (z + way * (hops - s) + 8) % 8
                value = u[b, target]
                if s > 0:
                    ring_copy(i, s - 1).wait_recv()
                    value = value + rbuf[i, s - 1]
                rsend[i, s] = value
                ring_copy(i, s).start()

    def exchange(j):
        cp = remote(xf.at[j, quarter, :], xf.at[j, quarter, :], h_send.at[j], h_recv.at[j], hdev)
        cp.start()
        sent.append(cp)
        swap[j] = cp

    def update(j):
        swap[j].wait_recv()
        if j == 0:
            for cp in (load_f, load_g):
                cp.wait()
            for cp in (pair[1], pair[3], pair[4]):
                cp.wait_recv()
        for b in range(2):
            part = dot3(xf[j], fv[j, :, b * 1024:(b + 1) * 1024], NN)
            for i in range(8):
                piece = part[:, i * 128:(i + 1) * 128]
                u[b, i] = piece if j == 0 else u[b, i] + piece

    for j in range(1, 5):
        stage = []
        for d in (4, 3, 5, 2, 6, 1, 7):
            cp = remote(ts.at[j], pa.at[j - 1, d - 1], a_send.at[j - 1, d], a_recv.at[j - 1, d], zdev(d))
            cp.start()
            stage.append(cp)
        sent.extend(stage)
        if j == 1:
            for cp in (pair[1], pair[3], pair[4]):
                cp.start()
                sent.append(cp)
            load_f.start()
            load_g.start()
            fwd[2] = forward(2)

            @pl.when(r != 0)
            def _():
                pltpu.make_async_copy(xf.at[0, quarter], xf.at[0, quarter], own_recv.at[0, 1]).wait()

            exchange(0)
            load_d.wait()
            pair[2].wait_recv()
        elif j < 4:
            fwd[j + 1] = forward(j + 1)
            if j == 2:
                update(0)
                update(1)
            else:
                update(2)
                spread_on()
        else:
            update(3)
            ring(0)
        hi, lo = halves(dv[j])
        dsplit[0] = hi
        dsplit[1] = lo
        for cp in stage:
            cp.wait_recv()
        total = ts[j]
        for d in range(7):
            total = total + pa[j - 1, d]
        rest = -total
        ss[j - 1] = rest
        sb[j - 1, g] = rest
        stage = []
        for dx in (2, 1, 3, 0):
            for dy in (1, 0):
                if dx == 0 and dy == 0:
                    continue
                ny = h * 2 + (y + dy) % 2
                to = {"rows": ((x + dx) % 4) * 4 + ny}
                k = dx * 2 + dy
                cp = remote(ss.at[j - 1], sb.at[j - 1, g], b_send.at[j - 1, k], b_recv.at[j - 1, k], to)
                cp.start()
                stage.append(cp)
        sent.extend(stage)
        if j == 4:
            ring(1)
        if j < 4:
            fwd[j + 1].wait_recv()
            part = dot3(xf[0, quarter, :], lts[j + 1][0], NN)
            for m in range(1, j):
                part = part + dot3(xf[m, quarter, :], lts[j + 1][m], NN)
            tp[...] = part
        for cp in stage:
            cp.wait_recv()
        rows = jnp.concatenate([sb[j - 1, i] for i in range(8)], axis=1)
        new = dot3_split(rows, dsplit[0], dsplit[1], NT)
        if j == 4:
            break
        xf[j, quarter, :] = new
        if j < 4:
            ts[j + 1] = tp[...] + dot3(new, lts[j + 1][j], NN)
            wait_jac(j + 1)

            @pl.when(z < 6)
            def _():
                ts[j + 1, subl(z, 8)] = ts[j + 1, subl(z, 8)] - jtile[j + 1]
        exchange(j)

    xz[h, z] = new

    def pass_on(i, k):
        cp = remote(xz.at[h, i], xz.at[h, i], x_send.at[k], x_recv.at[k], hdev)
        cp.start()
        sent.append(cp)
        return cp

    stage = {}
    for d in (4, 3, 5, 2, 6, 1, 7):
        cp = remote(xz.at[h, z], xz.at[h, z], x_send.at[8 + d], x_recv.at[8 + d], zdev(d))
        cp.start()
        sent.append(cp)
        stage[d] = cp
    passed = [pass_on(z, 0)]
    ring(2)
    for d in (1, 7, 2, 6, 3, 5, 4):
        stage[d].wait_recv()
        passed.append(pass_on((z - d + 8) % 8, d))
    ring(3)

    @pl.when(r >= 2)
    def _():
        spread_pair().wait_recv()

    right = jnp.concatenate(
        [jnp.concatenate([g4[k, i, b] for i in range(8) for k in range(2)], axis=0) for b in range(2)], axis=1
    )
    right_hi, right_lo = halves(right)
    for cp in passed:
        cp.wait_recv()
    xf[4] = jnp.concatenate([xz[0, z], xz[1, z]], axis=0)
    left = jnp.concatenate([jnp.concatenate([xz[k, i] for i in range(8)], axis=1) for k in range(2)], axis=0)
    tail = dot3_split(left, right_hi, right_lo, NN)

    def piece(b, origin):
        return og.at[b * 8 + origin]

    gather = {}

    def hop(b, k, origin, d):
        cp = remote(piece(b, origin), piece(b, origin), g_send.at[b, k], g_recv.at[b, k], zdev(d))
        cp.start()
        sent.append(cp)
        gather[b, k] = cp

    ways = (1, -1)

    @pl.when(r >= 2)
    def _():
        for i, (b, way, hops) in enumerate(paths):
            ring_copy(i, hops - 1).wait_recv()

    for b in range(2):
        first, second = [i for i in range(4) if paths[i][0] == b]
        total = tail[:, b * 128:(b + 1) * 128] + u[b, z] + rbuf[first, paths[first][2] - 1] + rbuf[second, paths[second][2] - 1]
        block = r * 2 + b
        solved = xf[jnp.minimum(block, 4)]
        updated = js[b] - total
        og[b * 8 + z] = jnp.where(block < 5, solved, updated)
        w = ways[b]
        for k, d in enumerate((2 * w, -2 * w, w, -w)):
            hop(b, k, z, d)
    done = [(0, z), (1, z)]
    shared = []

    def share():
        while done:
            b, origin = done.pop()
            p = b * 8 + origin
            k = len(shared)
            cp = remote(og.at[p], out.at[p, half], o_send.at[k], o_recv.at[k], partner)
            cp.start()
            sent.append(cp)
            shared.append(cp)

    def arrived(b, k, origin):
        gather[b, k].wait_recv()
        done.append((b, (origin + 16) % 8))

    for b in range(2):
        w = ways[b]
        arrived(b, 0, z - 2 * w)
        hop(b, 4, (z - 2 * w + 8) % 8, 2 * w)
        hop(b, 5, (z - 2 * w + 8) % 8, w)
    for b in range(2):
        w = ways[b]
        arrived(b, 1, z + 2 * w)
        hop(b, 6, (z + 2 * w + 8) % 8, -w)
    for b in range(2):
        w = ways[b]
        arrived(b, 2, z - w)
        arrived(b, 3, z + w)
    share()
    for b in range(2):
        w = ways[b]
        arrived(b, 6, z + 3 * w)
        arrived(b, 5, z - 3 * w)
        arrived(b, 4, z - 4 * w)
    share()
    keep = pltpu.make_async_copy(og, out.at[:, half], load_sem.at[8])
    keep.start()
    keep.wait()
    for cp in shared:
        cp.wait_recv()
    for cp in sent:
        cp.wait_send()

    @pl.when(r >= 2)
    def _():
        for d in range(1, 8):
            for b in range(2):
                spread_copy(d, b).wait_send()
        spread_pair().wait_send()
        for i, (b, way, hops) in enumerate(paths):
            for s in range(hops):
                ring_copy(i, s).wait_send()

    @pl.when(r == 0)
    def _():
        swap_t.wait_send()
        pair[0].wait_send()
        for d in range(1, 16):
            for cp in first_copy(d):
                cp.wait_send()

    @pl.when(r == 1)
    def _():
        wait_owner_sends(2)
        wait_owner_sends(3)

    @pl.when(r == 2)
    def _():
        wait_owner_sends(4)

    for j in (2, 3, 4):
        @pl.when(h == owner_h[j])
        def _():
            fac_pass(j).wait_send()


def per_device(jacobian, factor_cols, diag_inverse):
    f32 = jnp.float32
    dma = pltpu.SemaphoreType.DMA
    out = pl.pallas_call(
        kernel,
        out_shape=jax.ShapeDtypeStruct((16, 192, 128), f32),
        in_specs=[pl.BlockSpec(memory_space=pltpu.HBM)] * 3,
        out_specs=pl.BlockSpec(memory_space=pltpu.HBM),
        scratch_shapes=[
            pltpu.VMEM((5, 128, 1024), f32),
            pltpu.VMEM((4, 128, 2048), f32),
            pltpu.VMEM((192, 2048), f32),
            pltpu.VMEM((2, 96, 128), f32),
            pltpu.VMEM((96, 128), f32),
            pltpu.VMEM((8, 96, 128), f32),
            pltpu.VMEM((2, 8, 96, 128), f32),
            pltpu.VMEM((8, 96, 128), f32),
            pltpu.VMEM((6, 8, 64, 128), f32),
            pltpu.VMEM((5, 48, 128), f32),
            pltpu.VMEM((48, 128), f32),
            pltpu.VMEM((5, 96, 128), f32),
            pltpu.VMEM((2, 128, 128), f32),
            pltpu.VMEM((3, 128, 128), f32),
            pltpu.VMEM((4, 128, 128), f32),
            pltpu.VMEM((5, 8, 128), f32),
            pltpu.VMEM((4, 7, 48, 128), f32),
            pltpu.VMEM((4, 48, 128), f32),
            pltpu.VMEM((4, 8, 48, 128), f32),
            pltpu.VMEM((2, 8, 96, 128), f32),
            pltpu.VMEM((4, 4, 96, 128), f32),
            pltpu.VMEM((4, 4, 96, 128), f32),
            pltpu.VMEM((16, 96, 128), f32),
            pltpu.VMEM((2, 8, 2, 64, 128), f32),
            pltpu.VMEM((2, 8, 48, 128), f32),
            pltpu.VMEM((2, 128, 1024), jnp.bfloat16),
            dma((9,)),
            dma((6,)), dma((6,)),
            dma((5, 2, 16)), dma((5, 2)),
            dma((5,)), dma((5,)),
            dma((5,)), dma((5,)),
            dma((4, 8)), dma((4, 8)),
            dma((4, 8)), dma((4, 8)),
            dma((5,)), dma((5,)),
            dma((4, 4)), dma((4, 4)),
            dma((2, 8)), dma((2, 8)),
            dma((16,)), dma((16,)),
            dma((8, 2)), dma((9, 2)),
            dma((16,)), dma((16,)),
        ],
        compiler_params=pltpu.CompilerParams(
            collective_id=0, has_side_effects=True, vmem_limit_bytes=57 * 1024 * 1024
        ),
        name="whiten",
    )(jacobian.T, factor_cols, diag_inverse)
    return jnp.transpose(out, (0, 2, 1)).reshape(2048, 192)


def solution(mesh):
    in_specs = (P("rows", None), P(None, "cols", "rows"), P(None, "cols", None))
    return jax.shard_map(
        per_device, mesh=mesh, in_specs=in_specs, out_specs=P("rows", None), check_vma=False
    )
```

```python
import jax
import jax.numpy as jnp
from jax import lax
from jax.experimental import pallas as pl
from jax.experimental.pallas import tpu as pltpu
from jax.sharding import PartitionSpec as P

MESH = pl.DeviceIdType.MESH
FAR = (10, 8, 9, 11, 6, 5, 7, 4, 14, 13, 15, 12, 2, 1, 3)
NT = (((1,), (1,)), ((), ()))
NN = (((1,), (0,)), ((), ()))


def halves(a):
    hi = a.astype(jnp.bfloat16)
    lo = (a - hi.astype(jnp.float32)).astype(jnp.bfloat16)
    return hi, lo


def dot3(a, b, dims):
    ah, al = halves(a)
    bh, bl = halves(b)

    def one(p, q):
        return lax.dot_general(p, q, dims, preferred_element_type=jnp.float32)

    return one(ah, bh) + (one(ah, bl) + one(al, bh))


def dot3_split(a, bh, bl, dims):
    ah, al = halves(a)

    def one(p, q):
        return lax.dot_general(p, q, dims, preferred_element_type=jnp.float32)

    return one(ah, bh) + (one(ah, bl) + one(al, bh))


def lanes(i, n=128):
    return pl.ds(pl.multiple_of(i * n, n), n)


def subl(i, n):
    return pl.ds(pl.multiple_of(i * n, n), n)


def kernel(
    jac, fac, dinv, out,
    dv, fv, jt, js, x0, t1, tpart, tin, stage_f, ts, tp, xf, lt2, lt3, lt4, jtile,
    pa, ss, sb, u, rsend, rbuf, og, g4, xz, dsplit,
    load_sem, pair_send, pair_recv, own_send, own_recv, fwd_send, fwd_recv, pass_send, pass_recv,
    a_send, a_recv, b_send, b_recv, h_send, h_recv, r_send, r_recv, g_send, g_recv, o_send, o_recv, z_send, z_recv, x_send, x_recv,
):
    r = lax.axis_index("rows")
    c = lax.axis_index("cols")
    x = r // 4
    y = r % 4
    z = c // 2
    core = c % 2
    h = y // 2
    g = x * 2 + (y + h) % 2

    def zdev(d):
        return {"cols": ((z + d + 8) % 8) * 2 + core}

    def rdev(d):
        return {"rows": (r + d) % 16}

    partner = {"cols": c + 1 - 2 * core}
    hdev = {"rows": x * 4 + 3 - y}

    def remote(src, dst, ssem, rsem, dev):
        return pltpu.make_async_remote_copy(
            src_ref=src, dst_ref=dst, send_sem=ssem, recv_sem=rsem, device_id=dev, device_id_type=MESH
        )

    sent = []

    bar = pltpu.get_barrier_semaphore()
    for d in range(1, 16):
        pl.semaphore_signal(bar, inc=1, device_id=rdev(d), device_id_type=MESH)
    for d in range(1, 8):
        pl.semaphore_signal(bar, inc=1, device_id=zdev(d), device_id_type=MESH)
    pl.semaphore_signal(bar, inc=1, device_id=partner, device_id_type=MESH)

    mine = subl(core, 64)
    first_rows = pl.ds(1024, 1024)
    load_0 = [
        pltpu.make_async_copy(dinv.at[0], dv.at[0, mine, :], load_sem.at[0]),
        pltpu.make_async_copy(fac.at[0, :, first_rows], fv.at[0, mine, first_rows], load_sem.at[1]),
    ]
    load_d = pltpu.make_async_copy(dinv.at[pl.ds(1, 4)], dv.at[pl.ds(1, 4), mine, :], load_sem.at[5])
    load_f = pltpu.make_async_copy(fac.at[pl.ds(1, 3)], fv.at[pl.ds(1, 3), mine, :], load_sem.at[6])
    load_g = pltpu.make_async_copy(fac.at[0, :, pl.ds(0, 1024)], fv.at[0, mine, pl.ds(0, 1024)], load_sem.at[7])
    for cp in load_0:
        cp.start()
    load_j = [
        pltpu.make_async_copy(
            jac.at[subl(core, 96), pl.ds(pl.multiple_of(b * 1024 + z * 128, 128), 128)], js.at[b], load_sem.at[2 + b]
        )
        for b in range(2)
    ]
    for cp in load_j:
        cp.start()

    load_jt = pltpu.make_async_copy(jac, jt, load_sem.at[4])

    @pl.when(r == 0)
    def _():
        load_jt.start()
        for cp in load_0:
            cp.wait()
        load_jt.wait()
        first = dot3(jt[:, 0:1024], dv[0, mine, :], NT)
        whole = dot3(first, fv[0, mine, 1024:2048], NN)
        for i in range(8):
            for k in range(2):
                tpart[k, i] = whole[k * 96:(k + 1) * 96, i * 128:(i + 1) * 128]

        @pl.when(c == 0)
        def _():
            for i in range(8):
                for k in range(2):
                    tpart[k, i] = tpart[k, i] - jt[k * 96:(k + 1) * 96, 1024 + i * 128:1024 + (i + 1) * 128]

    lts = {2: lt2, 3: lt3, 4: lt4}
    owner_h = {2: 0, 3: 0, 4: 1}

    def fac_copy(j, k, fetch=False):
        tx = (x + k // 2) % 4
        ty = h * 2 + (y % 2 + k % 2) % 2
        tg = tx * 2 + (ty + h) % 2
        rows = pl.ds(pl.multiple_of((j % 2) * 1024 + tg * 128, 128), 128)
        dst = lts[j].at[:, mine, :]
        part = stage_f.at[pl.ds(0 if j == 4 else 3 * (j - 2), j), k]
        if fetch:
            return pltpu.make_async_copy(fac.at[pl.ds(0, j), :, rows], dst if k == 0 else part, own_send.at[j, 0, k] if k else own_recv.at[j, 0])
        return remote(part, dst, own_send.at[j, 0, k], own_recv.at[j, 0], {"rows": tx * 4 + ty})

    def jac_copy(j, d):
        to = (r + d) % 16
        tx = to // 4
        ty = to % 4
        th = ty // 2
        tg = tx * 2 + (ty + th) % 2
        rows = pl.ds(pl.multiple_of((j % 2) * 1024 + tg * 128, 128), 128)
        src = jac.at[pl.ds(pl.multiple_of(core * 96 + th * 48 + z * 8, 8), 8), rows]
        if d == 0:
            return pltpu.make_async_copy(src, jtile.at[j], own_recv.at[j, 1])
        return remote(src, jtile.at[j], own_send.at[j, 1, d], own_recv.at[j, 1], rdev(d))

    def fetch_fac(j):
        for k in (4, 5, 2, 3, 6, 7, 1, 0):
            fac_copy(j, k, True).start()

    def send_fac(j):
        for k in (4, 5, 2, 3, 6, 7, 1):
            fac_copy(j, k, True).wait()
            fac_copy(j, k).start()

    def send_jac(j):
        @pl.when(z < 6)
        def _():
            for d in range(16):
                jac_copy(j, d).start()

    def wait_fac(j):
        @pl.when(h == owner_h[j])
        def _():
            pltpu.make_async_copy(lts[j].at[:, mine, :], lts[j].at[:, mine, :], own_recv.at[j, 0]).wait()
            fac_pass(j).start()

        @pl.when(h != owner_h[j])
        def _():
            fac_pass(j).wait_recv()

    def fac_pass(j):
        return remote(lts[j].at[:, mine, :], lts[j].at[:, mine, :], pass_send.at[j], pass_recv.at[j], hdev)

    def wait_jac(j):
        @pl.when(z < 6)
        def _():
            pltpu.make_async_copy(jtile.at[j], jtile.at[j], own_recv.at[j, 1]).wait()

    def wait_owner_sends(j):
        for k in range(1, 8):
            fac_copy(j, k).wait_send()

        @pl.when(z < 6)
        def _():
            for d in range(1, 16):
                jac_copy(j, d).wait_send()

    @pl.when(r == 1)
    def _():
        fetch_fac(2)
        fetch_fac(3)

    @pl.when(r == 2)
    def _():
        fetch_fac(4)

    pl.semaphore_wait(bar, 23)
    swap_t = remote(tpart.at[1 - core], tin, pair_send.at[5], pair_recv.at[5], partner)

    @pl.when(r == 0)
    def _():
        swap_t.start()

    pair = [
        remote(src, dst, pair_send.at[i], pair_recv.at[i], partner)
        for i, (src, dst) in enumerate(
            (
                (dinv.at[0], dv.at[0, mine, :]),
                (fac.at[0, :, first_rows], fv.at[0, mine, first_rows]),
                (dinv.at[pl.ds(1, 4)], dv.at[pl.ds(1, 4), mine, :]),
                (fac.at[pl.ds(1, 3)], fv.at[pl.ds(1, 3), mine, :]),
                (fac.at[0, :, pl.ds(0, 1024)], fv.at[0, mine, pl.ds(0, 1024)]),
            )
        )
    ]

    @pl.when(r == 0)
    def _():
        pair[0].start()

    @pl.when(r == 1)
    def _():
        send_fac(2)
        send_jac(2)
        send_fac(3)
        send_jac(3)

    @pl.when(r == 2)
    def _():
        send_fac(4)
        send_jac(4)

    @pl.when(r != 0)
    def _():
        for cp in load_0:
            cp.wait()

    half = subl(core, 96)
    quarter = subl(h, 48)

    def first_copy(d):
        to = (r + d) % 16
        tx = to // 4
        ty = to % 4
        th = ty // 2
        tg = tx * 2 + (ty + th) % 2
        rows = pl.ds(pl.multiple_of(th * 48, 48), 48)
        t1_cp = remote(t1.at[tg, rows], ts.at[1], own_send.at[0, 0, d], own_recv.at[0, 0], rdev(d))
        x0_cp = remote(x0.at[rows], xf.at[0, rows], own_send.at[0, 1, d], own_recv.at[0, 1], rdev(d))
        return t1_cp, x0_cp

    @pl.when(r == 0)
    def _():
        swap_t.wait_recv()
        for i in range(8):
            t1[i] = tpart[core, i] + tin[i]
        for d in FAR:
            first_copy(d)[0].start()
        ts[1] = t1[0, 0:48]
        pair[0].wait_recv()
        x0[...] = dot3(jt[half, 0:1024], dv[0], NT)
        for d in FAR:
            first_copy(d)[1].start()
        xf[0, 0:48] = x0[0:48]

    def spread_copy(d, b):
        rows = lanes(b * 8 + (z + d) % 8)
        if d == 0:
            return pltpu.make_async_copy(fac.at[4, :, rows], g4.at[core, z, b], z_recv.at[0, b])
        return remote(fac.at[4, :, rows], g4.at[core, z, b], z_send.at[d, b], z_recv.at[d, b], zdev(d))

    def start_spread():
        @pl.when(r >= 2)
        def _():
            for d in (4, 3, 5, 2, 6, 1, 7, 0):
                for b in range(2):
                    spread_copy(d, b).start()

    start_spread()
    pair[2].start()
    sent.append(pair[2])
    load_d.start()
    for cp in load_j:
        cp.wait()

    @pl.when(r != 0)
    def _():
        pltpu.make_async_copy(ts.at[1], ts.at[1], own_recv.at[0, 0]).wait()

    def forward(j):
        wait_fac(j)
        cp = remote(lts[j].at[:, mine, :], lts[j].at[:, mine, :], fwd_send.at[j], fwd_recv.at[j], partner)
        cp.start()
        sent.append(cp)
        return cp

    fwd = {}
    swap = {}

    def spread_pair():
        return remote(g4.at[core], g4.at[core], z_send.at[0, 0], z_recv.at[8, 0], partner)

    def spread_on():
        @pl.when(r >= 2)
        def _():
            for d in range(8):
                for b in range(2):
                    if d:
                        spread_copy(d, b).wait_recv()
                    else:
                        spread_copy(d, b).wait()
            spread_pair().start()

    paths = ((0, -1, 4), (1, 1, 4), (0, 1, 3), (1, -1, 3))

    def ring_copy(i, s):
        b, way, hops = paths[i]
        return remote(rsend.at[i, s], rbuf.at[i, s], r_send.at[i, s], r_recv.at[i, s], zdev(way))

    def ring(s):
        @pl.when(r >= 2)
        def _():
            for i, (b, way, hops) in enumerate(paths):
                if s >= hops:
                    continue
                target = (z + way * (hops - s) + 8) % 8
                value = u[b, target]
                if s > 0:
                    ring_copy(i, s - 1).wait_recv()
                    value = value + rbuf[i, s - 1]
                rsend[i, s] = value
                ring_copy(i, s).start()

    def exchange(j):
        cp = remote(xf.at[j, quarter, :], xf.at[j, quarter, :], h_send.at[j], h_recv.at[j], hdev)
        cp.start()
        sent.append(cp)
        swap[j] = cp

    def update(j):
        swap[j].wait_recv()
        if j == 0:
            for cp in (load_f, load_g):
                cp.wait()
            for cp in (pair[1], pair[3], pair[4]):
                cp.wait_recv()
        for b in range(2):
            part = dot3(xf[j], fv[j, :, b * 1024:(b + 1) * 1024], NN)
            for i in range(8):
                piece = part[:, i * 128:(i + 1) * 128]
                u[b, i] = piece if j == 0 else u[b, i] + piece

    for j in range(1, 5):
        stage = []
        for d in (4, 3, 5, 2, 6, 1, 7):
            cp = remote(ts.at[j], pa.at[j - 1, d - 1], a_send.at[j - 1, d], a_recv.at[j - 1, d], zdev(d))
            cp.start()
            stage.append(cp)
        sent.extend(stage)
        if j == 1:
            for cp in (pair[1], pair[3], pair[4]):
                cp.start()
                sent.append(cp)
            load_f.start()
            load_g.start()
            fwd[2] = forward(2)

            @pl.when(r != 0)
            def _():
                pltpu.make_async_copy(xf.at[0, quarter], xf.at[0, quarter], own_recv.at[0, 1]).wait()

            exchange(0)
            load_d.wait()
            pair[2].wait_recv()
        elif j < 4:
            fwd[j + 1] = forward(j + 1)
            if j == 2:
                update(0)
                update(1)
            else:
                update(2)
                spread_on()
        else:
            update(3)
            ring(0)
        hi, lo = halves(dv[j])
        dsplit[0] = hi
        dsplit[1] = lo
        for cp in stage:
            cp.wait_recv()
        total = ts[j]
        for d in range(7):
            total = total + pa[j - 1, d]
        rest = -total
        ss[j - 1] = rest
        sb[j - 1, g] = rest
        stage = []
        for dx in (2, 1, 3, 0):
            for dy in (1, 0):
                if dx == 0 and dy == 0:
                    continue
                ny = h * 2 + (y + dy) % 2
                to = {"rows": ((x + dx) % 4) * 4 + ny}
                k = dx * 2 + dy
                cp = remote(ss.at[j - 1], sb.at[j - 1, g], b_send.at[j - 1, k], b_recv.at[j - 1, k], to)
                cp.start()
                stage.append(cp)
        sent.extend(stage)
        if j == 4:
            ring(1)
        if j < 4:
            fwd[j + 1].wait_recv()
            part = dot3(xf[0, quarter, :], lts[j + 1][0], NN)
            for m in range(1, j):
                part = part + dot3(xf[m, quarter, :], lts[j + 1][m], NN)
            tp[...] = part
        for cp in stage:
            cp.wait_recv()
        rows = jnp.concatenate([sb[j - 1, i] for i in range(8)], axis=1)
        new = dot3_split(rows, dsplit[0], dsplit[1], NT)
        if j == 4:
            break
        xf[j, quarter, :] = new
        if j < 4:
            ts[j + 1] = tp[...] + dot3(new, lts[j + 1][j], NN)
            wait_jac(j + 1)

            @pl.when(z < 6)
            def _():
                ts[j + 1, subl(z, 8)] = ts[j + 1, subl(z, 8)] - jtile[j + 1]
        exchange(j)

    xz[h, z] = new

    def pass_on(i, k):
        cp = remote(xz.at[h, i], xz.at[h, i], x_send.at[k], x_recv.at[k], hdev)
        cp.start()
        sent.append(cp)
        return cp

    stage = {}
    for d in (4, 3, 5, 2, 6, 1, 7):
        cp = remote(xz.at[h, z], xz.at[h, z], x_send.at[8 + d], x_recv.at[8 + d], zdev(d))
        cp.start()
        sent.append(cp)
        stage[d] = cp
    passed = [pass_on(z, 0)]
    ring(2)
    for d in (1, 7, 2, 6, 3, 5, 4):
        stage[d].wait_recv()
        passed.append(pass_on((z - d + 8) % 8, d))
    ring(3)

    @pl.when(r >= 2)
    def _():
        spread_pair().wait_recv()

    right = jnp.concatenate(
        [jnp.concatenate([g4[k, i, b] for i in range(8) for k in range(2)], axis=0) for b in range(2)], axis=1
    )
    right_hi, right_lo = halves(right)
    for cp in passed:
        cp.wait_recv()
    xf[4] = jnp.concatenate([xz[0, z], xz[1, z]], axis=0)
    left = jnp.concatenate([jnp.concatenate([xz[k, i] for i in range(8)], axis=1) for k in range(2)], axis=0)
    tail = dot3_split(left, right_hi, right_lo, NN)

    def piece(b, origin):
        return og.at[b * 8 + origin]

    gather = {}

    def hop(b, k, origin, d):
        cp = remote(piece(b, origin), piece(b, origin), g_send.at[b, k], g_recv.at[b, k], zdev(d))
        cp.start()
        sent.append(cp)
        gather[b, k] = cp

    ways = (1, -1)

    @pl.when(r >= 2)
    def _():
        for i, (b, way, hops) in enumerate(paths):
            ring_copy(i, hops - 1).wait_recv()

    for b in range(2):
        first, second = [i for i in range(4) if paths[i][0] == b]
        total = tail[:, b * 128:(b + 1) * 128] + u[b, z] + rbuf[first, paths[first][2] - 1] + rbuf[second, paths[second][2] - 1]
        block = r * 2 + b
        solved = xf[jnp.minimum(block, 4)]
        updated = js[b] - total
        og[b * 8 + z] = jnp.where(block < 5, solved, updated)
        w = ways[b]
        for k, d in enumerate((2 * w, -2 * w)):
            hop(b, k, z, d)
    for b in range(2):
        w = ways[b]
        for k, d in enumerate((w, -w)):
            hop(b, 2 + k, z, d)
    done = [(0, z), (1, z)]
    shared = []

    def share():
        while done:
            b, origin = done.pop()
            p = b * 8 + origin
            k = len(shared)
            cp = remote(og.at[p], out.at[p, half], o_send.at[k], o_recv.at[k], partner)
            cp.start()
            sent.append(cp)
            shared.append(cp)

    def arrived(b, k, origin):
        gather[b, k].wait_recv()
        done.append((b, (origin + 16) % 8))

    for b in range(2):
        w = ways[b]
        arrived(b, 0, z - 2 * w)
        hop(b, 4, (z - 2 * w + 8) % 8, 2 * w)
        hop(b, 5, (z - 2 * w + 8) % 8, w)
    for b in range(2):
        w = ways[b]
        arrived(b, 1, z + 2 * w)
        hop(b, 6, (z + 2 * w + 8) % 8, -w)
    for b in range(2):
        w = ways[b]
        arrived(b, 2, z - w)
        arrived(b, 3, z + w)
    share()
    for b in range(2):
        w = ways[b]
        arrived(b, 6, z + 3 * w)
        arrived(b, 5, z - 3 * w)
        arrived(b, 4, z - 4 * w)
    share()
    keep = pltpu.make_async_copy(og, out.at[:, half], load_sem.at[8])
    keep.start()
    keep.wait()
    for cp in shared:
        cp.wait_recv()
    for cp in sent:
        cp.wait_send()

    @pl.when(r >= 2)
    def _():
        for d in range(1, 8):
            for b in range(2):
                spread_copy(d, b).wait_send()
        spread_pair().wait_send()
        for i, (b, way, hops) in enumerate(paths):
            for s in range(hops):
                ring_copy(i, s).wait_send()

    @pl.when(r == 0)
    def _():
        swap_t.wait_send()
        pair[0].wait_send()
        for d in range(1, 16):
            for cp in first_copy(d):
                cp.wait_send()

    @pl.when(r == 1)
    def _():
        wait_owner_sends(2)
        wait_owner_sends(3)

    @pl.when(r == 2)
    def _():
        wait_owner_sends(4)

    for j in (2, 3, 4):
        @pl.when(h == owner_h[j])
        def _():
            fac_pass(j).wait_send()


def per_device(jacobian, factor_cols, diag_inverse):
    f32 = jnp.float32
    dma = pltpu.SemaphoreType.DMA
    out = pl.pallas_call(
        kernel,
        out_shape=jax.ShapeDtypeStruct((16, 192, 128), f32),
        in_specs=[pl.BlockSpec(memory_space=pltpu.HBM)] * 3,
        out_specs=pl.BlockSpec(memory_space=pltpu.HBM),
        scratch_shapes=[
            pltpu.VMEM((5, 128, 1024), f32),
            pltpu.VMEM((4, 128, 2048), f32),
            pltpu.VMEM((192, 2048), f32),
            pltpu.VMEM((2, 96, 128), f32),
            pltpu.VMEM((96, 128), f32),
            pltpu.VMEM((8, 96, 128), f32),
            pltpu.VMEM((2, 8, 96, 128), f32),
            pltpu.VMEM((8, 96, 128), f32),
            pltpu.VMEM((6, 8, 64, 128), f32),
            pltpu.VMEM((5, 48, 128), f32),
            pltpu.VMEM((48, 128), f32),
            pltpu.VMEM((5, 96, 128), f32),
            pltpu.VMEM((2, 128, 128), f32),
            pltpu.VMEM((3, 128, 128), f32),
            pltpu.VMEM((4, 128, 128), f32),
            pltpu.VMEM((5, 8, 128), f32),
            pltpu.VMEM((4, 7, 48, 128), f32),
            pltpu.VMEM((4, 48, 128), f32),
            pltpu.VMEM((4, 8, 48, 128), f32),
            pltpu.VMEM((2, 8, 96, 128), f32),
            pltpu.VMEM((4, 4, 96, 128), f32),
            pltpu.VMEM((4, 4, 96, 128), f32),
            pltpu.VMEM((16, 96, 128), f32),
            pltpu.VMEM((2, 8, 2, 64, 128), f32),
            pltpu.VMEM((2, 8, 48, 128), f32),
            pltpu.VMEM((2, 128, 1024), jnp.bfloat16),
            dma((9,)),
            dma((6,)), dma((6,)),
            dma((5, 2, 16)), dma((5, 2)),
            dma((5,)), dma((5,)),
            dma((5,)), dma((5,)),
            dma((4, 8)), dma((4, 8)),
            dma((4, 8)), dma((4, 8)),
            dma((5,)), dma((5,)),
            dma((4, 4)), dma((4, 4)),
            dma((2, 8)), dma((2, 8)),
            dma((16,)), dma((16,)),
            dma((8, 2)), dma((9, 2)),
            dma((16,)), dma((16,)),
        ],
        compiler_params=pltpu.CompilerParams(
            collective_id=0, has_side_effects=True, vmem_limit_bytes=57 * 1024 * 1024
        ),
        name="whiten",
    )(jacobian.T, factor_cols, diag_inverse)
    return jnp.transpose(out, (0, 2, 1)).reshape(2048, 192)


def solution(mesh):
    in_specs = (P("rows", None), P(None, "cols", "rows"), P(None, "cols", None))
    return jax.shard_map(
        per_device, mesh=mesh, in_specs=in_specs, out_specs=P("rows", None), check_vma=False
    )
```
